128 devices in a mesh: surf: 128 (over z, y, x, core).
Axes of the slice: x: 4, y: 4, z: 4, core: 2. Of those that a mesh axis runs over, the one named last changes fastest.
Arguments:
- splat: float32 [11, 524288], P(None, 'surf'), may hold values from -4 to 4
- position: float32 [3, 524288], P(None, 'surf'), may hold values from -3 to 3
- harmonics: float32 [48, 524288], P(None, 'surf'), may hold values from -2 to 2
- cameras: float32 [4, 3], replicated, may hold values from 5 to 8
- tile_lists: int32 [4096, 256], P('surf'), may hold values from 0 to 524287, as said below
- tile_counts: int32 [4096], P('surf'), may hold values from 1 to 256, as said below
- target_color: float32 [3, 4096, 256], P(None, 'surf'), may hold values from 0 to 1
- target_normal: float32 [3, 4096, 256], P(None, 'surf'), may hold values from -3 to 3
Outputs:
- grad_splat: float32 [11, 524288], P(None, 'surf')
- grad_position: float32 [3, 524288], P(None, 'surf')
- grad_harmonics: float32 [48, 524288], P(None, 'surf')
- tile_loss: float32 [4096], P('surf')
The draws below stay inside these ranges and needn't reach their ends.
Inputs may be any that keep to these rules, and one draw needn't show every extreme that they name: `tile_lists`: entries name surfels; among the live slots of the tiles of one device, exactly 32 * 192 / 128 name surfels of each block of 4096 consecutive surfel numbers, and among its padding slots exactly 32 * 64 / 128. `tile_counts`: the counts of one device's tiles sum to 6144; one tile of every device is full.
All inputs are finite; a program needn't handle non-finite values.
Results may differ from the reference program's by a relative error of at most 0.0003.
Values sent between devices are 32-bit elements; how exact they have to be, the bound alone decides.
A program may use at most 128 MiB of HBM per device.

```python
import jax
import jax.numpy as jnp
from jax import lax

TILES_DEV = 32
SURF_DEV = 4096
TILES = 4096
SURFELS = 524288


def slot_layout(key):
    blocks = TILES // TILES_DEV
    rest = TILES_DEV - 1
    room = rest * 255
    extra = TILES_DEV * 192 - 256 - rest
    slots = TILES_DEV * 256
    live_share = TILES_DEV * 192 // blocks
    pad_share = TILES_DEV * 64 // blocks

    def one_device(device_key):
        count_key, live_key, pad_key, local_key, order_key = jax.random.split(device_key, 5)
        marks = (jax.random.permutation(count_key, room) < extra).astype(jnp.int32)
        ordered = jnp.concatenate([jnp.full((1,), 256, jnp.int32), 1 + jnp.sum(marks.reshape(rest, 255), axis=1).astype(jnp.int32)])
        counts = ordered[jax.random.permutation(order_key, TILES_DEV)]
        live = (jnp.arange(256, dtype=jnp.int32)[None, :] < counts[:, None]).reshape(slots)
        live_int = live.astype(jnp.int32)
        live_rank = jnp.clip(jnp.cumsum(live_int) - 1, 0, blocks * live_share - 1).astype(jnp.int32)
        pad_rank = jnp.clip(jnp.cumsum(1 - live_int) - 1, 0, blocks * pad_share - 1).astype(jnp.int32)
        live_holders = jax.random.permutation(live_key, jnp.repeat(jnp.arange(blocks, dtype=jnp.int32), live_share))
        pad_holders = jax.random.permutation(pad_key, jnp.repeat(jnp.arange(blocks, dtype=jnp.int32), pad_share))
        holder = jnp.where(live, live_holders[live_rank], pad_holders[pad_rank])
        local = jax.random.randint(local_key, (slots,), 0, SURF_DEV, dtype=jnp.int32)
        return (counts, (holder * SURF_DEV + local).reshape(TILES_DEV, 256))
    keys = jax.random.split(key, blocks)
    counts, lists = jax.vmap(one_device)(keys)
    return (counts.reshape(TILES).astype(jnp.int32), lists.reshape(TILES, 256).astype(jnp.int32))


def draw_tile_lists(key, part):
    shared = slot_layout(key)
    return shared[1]


def draw_tile_counts(key, part):
    shared = slot_layout(key)
    return shared[0]


def draw_splat(key, part):
    key = jax.random.fold_in(key, 5)
    shape_key, offset_key, slope_key, opacity_key = jax.random.split(key, 4)
    slopes = jax.random.uniform(slope_key, (4, SURFELS), jnp.float32, -4.0, 4.0)
    rows = jnp.clip(jax.random.normal(shape_key, (11, SURFELS), jnp.float32), -4.0, 4.0)
    offsets = 1.5 * jnp.clip(jax.random.normal(offset_key, (2, SURFELS), jnp.float32), -2.6, 2.6)
    opacity = -2.2 + 0.6 * jnp.clip(jax.random.normal(opacity_key, (SURFELS,), jnp.float32), -3.0, 3.0)
    rows = rows.at[0].set(offsets[0]).at[3].set(offsets[1])
    rows = rows.at[1].set(slopes[0]).at[2].set(slopes[1]).at[4].set(slopes[2]).at[5].set(slopes[3])
    return rows.at[6].set(opacity).astype(jnp.float32)


def block_scale(stream_key, dims, cuts, low, high):
    def one(dim, blocks):
        draws = jax.random.uniform(jax.random.fold_in(jax.random.fold_in(stream_key, 6), dim), (blocks,), jnp.float32, low / len(cuts), high / len(cuts))
        return jnp.repeat(jnp.exp(draws), dims[dim] // blocks).reshape((-1,) + (1,) * (len(dims) - dim - 1))

    factor_of = one(*cuts[0])
    for cut in cuts[1:]:
        factor_of = factor_of * one(*cut)
    return factor_of


def noise(own_key, extent, deviation, most, cuts=(), kind=jnp.bfloat16):
    drawn = deviation * jax.random.normal(own_key, extent, jnp.float32)
    if cuts:
        drawn = drawn * block_scale(own_key, extent, cuts, -0.22, 0.18)
    return jnp.clip(drawn, -most, most).astype(kind)


def setup_inputs(seed: int = 0) -> dict:
    streams_of = jax.random.split(jax.random.key(seed), 9)
    return {
        "splat": draw_splat(jax.random.fold_in(streams_of[8], 71), 0),
        "position": noise(streams_of[1], (3, SURFELS), 1.0, 3.0, ((1, 128),), jnp.float32),
        "harmonics": noise(streams_of[2], (48, SURFELS), 0.3, 2.0, ((1, 128),), jnp.float32),
        "cameras": jnp.clip(jax.random.uniform(streams_of[3], (4, 3), jnp.float32, 5.0, 8.0), 5.0, 8.0),
        "tile_lists": draw_tile_lists(jax.random.fold_in(streams_of[8], 71), 0),
        "tile_counts": draw_tile_counts(jax.random.fold_in(streams_of[8], 71), 0),
        "target_color": jnp.clip(1.0 * jax.random.uniform(streams_of[6], (3, TILES, 256), jnp.float32) ** block_scale(streams_of[6], (3, TILES, 256), ((1, 128),), -0.2, 0.2), 0.0, 1.0),
        "target_normal": noise(streams_of[7], (3, TILES, 256), 0.6, 3.0, ((1, 128),), jnp.float32),
    }


sh_zero = 0.28209479177387814
sh_one = 0.4886025119029199
sh_two = (1.0925484305920792, -1.0925484305920792, 0.31539156525252005, -1.0925484305920792, 0.5462742152960396)
sh_three = (-0.5900435899266435, 2.890611442640554, -0.4570457994644658, 0.3731763325901154, -0.4570457994644658, 1.445305721320277, -0.5900435899266435)

def sh_color(centre, coeffs, camera):
    offset = centre - camera
    length = jnp.sqrt(lax.optimization_barrier(jnp.sum(offset * offset, axis=0)))
    xdir = offset[0] / length
    ydir = offset[1] / length
    zdir = offset[2] / length
    xsq = xdir * xdir
    ysq = ydir * ydir
    zsq = zdir * zdir
    basis = jnp.stack([jnp.full_like(xdir, sh_zero), -sh_one * ydir, sh_one * zdir, -sh_one * xdir, sh_two[0] * xdir * ydir, sh_two[1] * ydir * zdir, sh_two[2] * (2.0 * zsq - xsq - ysq), sh_two[3] * xdir * zdir, sh_two[4] * (xsq - ysq), sh_three[0] * ydir * (3.0 * xsq - ysq), sh_three[1] * xdir * ydir * zdir, sh_three[2] * ydir * (4.0 * zsq - xsq - ysq), sh_three[3] * zdir * (2.0 * zsq - 3.0 * xsq - 3.0 * ysq), sh_three[4] * xdir * (4.0 * zsq - xsq - ysq), sh_three[5] * zdir * (xsq - ysq), sh_three[6] * xdir * (xsq - 3.0 * ysq)], axis=0)
    shaped = coeffs.reshape(3, 16, coeffs.shape[-1])
    return jnp.maximum(lax.optimization_barrier(jnp.sum(shaped * basis[None], axis=1)) + 0.5, 0.0)

def pick_camera(cameras, view):
    chosen = jnp.zeros((3, view.shape[0]), cameras.dtype)
    for which in range(4):
        chosen = jnp.where(view[None, :] == which, cameras[which][:, None], chosen)
    return chosen

def tile_loss_of(geom, colors, count, target, normals):
    pixel = jnp.arange(256, dtype=jnp.int32)
    px = ((pixel % 16).astype(geom.dtype) - 7.5) / 8.0
    py = ((pixel // 16).astype(geom.dtype) - 7.5) / 8.0
    ucoord = geom[0][None, :] + geom[1][None, :] * px[:, None] + geom[2][None, :] * py[:, None]
    vcoord = geom[3][None, :] + geom[4][None, :] * px[:, None] + geom[5][None, :] * py[:, None]
    live = (jnp.arange(256, dtype=jnp.int32) < count).astype(geom.dtype)
    alpha = (live * 0.95 * jax.nn.sigmoid(geom[6]))[None, :] * jnp.exp(-0.5 * (ucoord * ucoord + vcoord * vcoord))
    logkeep = jnp.log(1.0 - alpha)
    trans = jnp.exp(jnp.cumsum(logkeep, axis=1) - logkeep)
    weight = alpha * trans
    render = jnp.einsum('pk,ck->cp', weight, colors, precision=lax.Precision.HIGHEST)
    color_term = jnp.sum((render - target) ** 2) / 256.0
    depth = geom[7][None, :]
    wdepth = weight * depth
    before_w = jnp.cumsum(weight, axis=1) - weight
    before_wd = jnp.cumsum(wdepth, axis=1) - wdepth
    distortion = jnp.sum(2.0 * weight * (depth * before_w - before_wd)) / 256.0
    facing = jnp.einsum('cp,ck->pk', normals, geom[8:11], precision=lax.Precision.HIGHEST)
    normal_term = jnp.sum(weight * (1.0 - facing)) / 256.0
    return color_term + distortion + 0.5 * normal_term

def reference(splat, position, harmonics, cameras, tile_lists, tile_counts, target_color, target_normal):
    tile_grad = jax.value_and_grad(tile_loss_of, argnums=(0, 1))
    slots = TILES * 256
    flat = tile_lists.reshape(-1)
    slot_view = (jnp.arange(slots, dtype=jnp.int32) // 256 // (TILES // 4)).astype(jnp.int32)
    geom = splat[:, flat]
    colors, color_back = jax.vjp(sh_color, position[:, flat], harmonics[:, flat], pick_camera(cameras, slot_view))
    geom_t = jnp.transpose(geom.reshape(11, TILES, 256), (1, 0, 2))
    col_t = jnp.transpose(colors.reshape(3, TILES, 256), (1, 0, 2))
    target_t = jnp.transpose(target_color, (1, 0, 2))
    normal_t = jnp.transpose(target_normal, (1, 0, 2))

    def one_tile(items):
        value, grads = tile_grad(items[0], items[1], items[2], items[3], items[4])
        return (value, grads[0], grads[1])
    losses, dgeom, dcol = lax.map(one_tile, (geom_t, col_t, tile_counts, target_t, normal_t))
    dgeom = jnp.transpose(dgeom, (1, 0, 2)).reshape(11, slots)
    dcol = jnp.transpose(dcol, (1, 0, 2)).reshape(3, slots)
    dpos, dsh, unused = color_back(dcol)
    grad_splat = jnp.zeros((11, SURFELS), splat.dtype).at[:, flat].add(dgeom)
    grad_position = jnp.zeros((3, SURFELS), splat.dtype).at[:, flat].add(dpos)
    grad_harmonics = jnp.zeros((48, SURFELS), splat.dtype).at[:, flat].add(dsh)
    return (grad_splat, grad_position, grad_harmonics, losses)
```

```python
import functools

import jax
import jax.numpy as jnp
from jax import lax
from jax.experimental import pallas as pl
from jax.experimental.pallas import tpu as pltpu
from jax.sharding import PartitionSpec as P

F32 = jnp.float32
BF16 = jnp.bfloat16
I32 = jnp.int32
MESH = pl.DeviceIdType.MESH
N_DEV = 128
TILES = 32
SURF = 4096
SHARE = 48
LOG2E = 1.4426950408889634

sh_zero = 0.28209479177387814
sh_one = 0.4886025119029199
sh_two = (
    1.0925484305920792,
    -1.0925484305920792,
    0.31539156525252005,
    -1.0925484305920792,
    0.5462742152960396,
)
sh_three = (
    -0.5900435899266435,
    2.890611442640554,
    -0.4570457994644658,
    0.3731763325901154,
    -0.4570457994644658,
    1.445305721320277,
    -0.5900435899266435,
)


def iota(shape, dim):
    return lax.broadcasted_iota(I32, shape, dim)


def dot_nn(a, b):
    return lax.dot_general(a, b, (((1,), (0,)), ((), ())), preferred_element_type=F32)


def dot_nt(a, b):
    return lax.dot_general(a, b, (((1,), (1,)), ((), ())), preferred_element_type=F32)


def dot_tn(a, b):
    return lax.dot_general(a, b, (((0,), (0,)), ((), ())), preferred_element_type=F32)


def split2(x):
    hi = x.astype(BF16)
    return hi, (x - hi.astype(F32)).astype(BF16)


def split3(x):
    hi = x.astype(BF16)
    rest = x - hi.astype(F32)
    mid = rest.astype(BF16)
    return hi, mid, (rest - mid.astype(F32)).astype(BF16)


def one_hot_rows(rows, index):
    return jnp.where(iota((rows, index.shape[1]), 0) == index, 1.0, 0.0).astype(BF16)


def directions(pos_rows, cams):
    offs = [pos_rows[d] - cams[:, d : d + 1] for d in range(3)]
    length = jnp.sqrt(offs[0] * offs[0] + offs[1] * offs[1] + offs[2] * offs[2])
    return [o / length for o in offs], length


def sh_basis(x, y, z):
    xx, yy, zz = x * x, y * y, z * z
    t, h = sh_two, sh_three
    return [
        jnp.full_like(x, sh_zero),
        -sh_one * y,
        sh_one * z,
        -sh_one * x,
        t[0] * (x * y),
        t[1] * (y * z),
        t[2] * (2.0 * zz - xx - yy),
        t[3] * (x * z),
        t[4] * (xx - yy),
        h[0] * (y * (3.0 * xx - yy)),
        h[1] * (x * y * z),
        h[2] * (y * (4.0 * zz - xx - yy)),
        h[3] * (z * (2.0 * zz - 3.0 * xx - 3.0 * yy)),
        h[4] * (x * (4.0 * zz - xx - yy)),
        h[5] * (z * (xx - yy)),
        h[6] * (x * (xx - 3.0 * yy)),
    ]


def sh_basis_back(x, y, z, d):
    xx, yy, zz = x * x, y * y, z * z
    xy, yz, xz = x * y, y * z, x * z
    t, h = sh_two, sh_three
    gx = (
        -sh_one * d[3] + t[0] * (y * d[4]) - (2.0 * t[2]) * (x * d[6]) + t[3] * (z * d[7])
        + (2.0 * t[4]) * (x * d[8]) + (6.0 * h[0]) * (xy * d[9]) + h[1] * (yz * d[10])
        - (2.0 * h[2]) * (xy * d[11]) - (6.0 * h[3]) * (xz * d[12])
        + h[4] * ((4.0 * zz - 3.0 * xx - yy) * d[13]) + (2.0 * h[5]) * (xz * d[14])
        + (3.0 * h[6]) * ((xx - yy) * d[15])
    )
    gy = (
        -sh_one * d[1] + t[0] * (x * d[4]) + t[1] * (z * d[5]) - (2.0 * t[2]) * (y * d[6])
        - (2.0 * t[4]) * (y * d[8]) + (3.0 * h[0]) * ((xx - yy) * d[9]) + h[1] * (xz * d[10])
        + h[2] * ((4.0 * zz - xx - 3.0 * yy) * d[11]) - (6.0 * h[3]) * (yz * d[12])
        - (2.0 * h[4]) * (xy * d[13]) - (2.0 * h[5]) * (yz * d[14]) - (6.0 * h[6]) * (xy * d[15])
    )
    gz = (
        sh_one * d[2] + t[1] * (y * d[5]) + (4.0 * t[2]) * (z * d[6]) + t[3] * (x * d[7])
        + h[1] * (xy * d[10]) + (8.0 * h[2]) * (yz * d[11])
        + h[3] * ((6.0 * zz - 3.0 * xx - 3.0 * yy) * d[12]) + (8.0 * h[4]) * (xz * d[13])
        + h[5] * ((xx - yy) * d[14])
    )
    return gx, gy, gz


def route_kernel(lists_ref, counts_ref, send_ref, pos_ref, upper):
    upper[...] = jnp.where(iota((256, 256), 0) < iota((256, 256), 1), 1.0, 0.0).astype(BF16)
    holder_id = iota((N_DEV, 256), 0)
    lane = iota((1, 256), 1)

    def tile(t, state):
        carry, acc_hi, acc_lo = state
        flat = lists_ref[pl.ds(t, 1), :]
        live = lane < counts_ref[t]
        holder = jnp.where(live, flat // SURF, -1)
        local = flat % SURF
        mine = holder_id == holder
        ones = jnp.where(mine, 1.0, 0.0)
        count = dot_nn(ones.astype(BF16), upper[...]) + carry
        rank = jnp.sum(ones * count, axis=0, keepdims=True).astype(I32)
        pos_ref[pl.ds(t, 1), :] = jnp.where(live, holder * 64 + rank, -1)
        hi = jnp.where(mine, (local // 64).astype(F32), 0.0).astype(BF16)
        lo = jnp.where(mine, (local % 64).astype(F32), 0.0).astype(BF16)
        rank_hot = jnp.where((iota((N_DEV, 256), 0) & 63) == rank, 1.0, 0.0).astype(BF16)
        carry = carry + jnp.sum(ones, axis=1, keepdims=True)
        return carry, acc_hi + dot_nt(hi, rank_hot), acc_lo + dot_nt(lo, rank_hot)

    zero = jnp.zeros((N_DEV, 128), F32)
    _, acc_hi, acc_lo = lax.fori_loop(0, TILES, tile, (jnp.zeros((N_DEV, 1), F32), zero, zero))
    local = (acc_hi * 64.0 + acc_lo).astype(I32)
    send_ref[:, 0, :] = jnp.where((iota((N_DEV, 128), 1) & 63) < SHARE, local, -1)


def exchange_kernel(x_ref, o_ref, send_sem, recv_sem, own_sem):
    me = lax.axis_index("surf")
    barrier = pltpu.get_barrier_semaphore()

    def greet(i, c):
        pl.semaphore_signal(
            barrier, inc=1, device_id=(lax.rem(me + i, N_DEV),), device_id_type=MESH
        )
        return c

    lax.fori_loop(1, N_DEV, greet, 0)
    own = pltpu.make_async_copy(x_ref.at[me], o_ref.at[me], own_sem)
    own.start()
    pl.semaphore_wait(barrier, N_DEV - 1)

    def send(i, c):
        peer = lax.rem(me + i, N_DEV)
        pltpu.make_async_remote_copy(
            src_ref=x_ref.at[peer],
            dst_ref=o_ref.at[me],
            send_sem=send_sem,
            recv_sem=recv_sem,
            device_id=(peer,),
            device_id_type=MESH,
        ).start()
        return c

    lax.fori_loop(1, N_DEV, send, 0)
    own.wait()
    pltpu.make_async_remote_copy(
        src_ref=x_ref.at[pl.ds(0, N_DEV - 1)],
        dst_ref=o_ref.at[pl.ds(0, N_DEV - 1)],
        send_sem=send_sem,
        recv_sem=recv_sem,
        device_id=(me,),
        device_id_type=MESH,
    ).wait()


def pair_lanes(even, odd):
    return jnp.where(iota(even.shape, 1) < 64, even, odd)


def fetch_index(got_ref, q):
    rows = [got_ref[4 * q + i] for i in range(4)]
    return jnp.concatenate([pair_lanes(rows[0], rows[1]), pair_lanes(rows[2], rows[3])], axis=1)


def pack_pair(g, out_ref, first):
    top, low = g[0:8], g[8:16]
    out_ref[first] = pair_lanes(top, pltpu.roll(low, 64, 1))
    out_ref[first + 1] = pair_lanes(pltpu.roll(top, 64, 1), low)


def unpack_pair(in_ref, first):
    even, odd = in_ref[first], in_ref[first + 1]
    return jnp.concatenate(
        [pair_lanes(even, pltpu.roll(odd, 64, 1)), pair_lanes(pltpu.roll(even, 64, 1), odd)], axis=0
    )


def gather_kernel(splat_ref, position_ref, harmonics_ref, cams_ref, got_ref, out_ref, table):
    cams = cams_ref[...]

    def build(h, c):
        lanes = pl.ds(pl.multiple_of(h * 256, 256), 256)
        (x, y, z), _ = directions([position_ref[d : d + 1, lanes] for d in range(3)], cams)
        basis = sh_basis(x, y, z)
        colors = []
        for ch in range(3):
            total = jnp.zeros_like(x)
            for b in range(16):
                total = total + harmonics_ref[ch * 16 + b : ch * 16 + b + 1, lanes] * basis[b]
            colors.append(jnp.maximum(total + 0.5, 0.0))
        splat = splat_ref[:, lanes]
        for v in range(4):
            rows = jnp.concatenate(
                [splat] + [col[v : v + 1] for col in colors] + [jnp.zeros((2, 256), F32)], axis=0
            )
            table[v, pl.ds(pl.multiple_of(h * 16, 16), 16), :] = jnp.concatenate(split3(rows), axis=1)
        return c

    lax.fori_loop(0, 16, build, 0)

    def fetch(q, c):
        index = fetch_index(got_ref, q)
        hot = one_hot_rows(256, index & 255)
        found = dot_nn(table[q // 8], jnp.concatenate([hot, hot, hot], axis=0))
        high = index >> 8
        g = jnp.zeros((16, 256), F32)
        for h in range(16):
            g = g + jnp.where(high == h, found[h * 16 : h * 16 + 16], 0.0)
        pack_pair(g[:, 0:128], out_ref, 4 * q)
        pack_pair(g[:, 128:256], out_ref, 4 * q + 2)
        return c

    lax.fori_loop(0, 32, fetch, 0)


def tiles_kernel(
    recv_ref, pos_ref, counts_ref, color_ref, normal_ref, loss_ref, out_ref,
    table, acc, before, sign, after, mono_col, mono_row,
):
    for q in range(32):
        for half in range(2):
            g = unpack_pair(recv_ref, 4 * q + 2 * half)
            for s, part in enumerate(split3(g)):
                table[q * 16 : q * 16 + 16, s * 256 + half * 128 : s * 256 + half * 128 + 128] = part
    acc[...] = jnp.zeros_like(acc)
    j, k = iota((512, 256), 0) & 255, iota((512, 256), 1)
    before[...] = jnp.where(j < k, 1.0, 0.0).astype(BF16)
    sign[...] = jnp.where(j < k, 1.0, jnp.where(j > k, -1.0, 0.0)).astype(BF16)
    after[...] = jnp.where(j > k, 1.0, 0.0).astype(BF16)

    def monomials(pixel, which):
        px = ((pixel & 15).astype(F32) - 7.5) * 0.125
        py = ((pixel >> 4).astype(F32) - 7.5) * 0.125
        m = jnp.where(which == 0, 1.0, 0.0)
        for n, value in ((1, px), (2, py), (3, px * px), (4, px * py), (5, py * py)):
            m = jnp.where(which == n, value, m)
        return m

    col = iota((256, 128), 1)
    mono_col[...] = jnp.where(
        col < 24, monomials(iota((256, 128), 0), col & 7), 0.0
    ).astype(BF16)
    mono_row[...] = monomials(iota((16, 512), 1) & 255, iota((16, 512), 0)).astype(BF16)

    lane = iota((1, 256), 1)
    row8 = iota((8, 256), 0)
    y_scale = jnp.where(row8 < 3, -0.25, jnp.where(row8 < 6, 1.0, 0.0))
    y_const = jnp.where(row8 == 6, 0.25, 0.0)
    zero1 = jnp.zeros((1, 256), F32)
    zero8 = jnp.zeros((8, 256), F32)
    kappa = 2.0 / 256.0

    def tile(t, c):
        index = pos_ref[pl.ds(t, 1), :]
        live = lane < counts_ref[t]
        high = index >> 8
        hot = one_hot_rows(256, index & 255)
        found = dot_nn(table[...], jnp.concatenate([hot, hot, hot], axis=0))
        g = jnp.zeros((16, 256), F32)
        for h in range(32):
            g = g + jnp.where(high == h, found[h * 16 : h * 16 + 16], 0.0)
        a0, a1, a2, b0, b1, b2, logit, depth = [g[r : r + 1] for r in range(8)]
        v8 = g[8:16]

        s = -0.5 * LOG2E
        grow = jnp.exp(-logit)
        offset = jnp.log(1.0 + grow) * (-LOG2E) + (-0.07400058144377693)
        sig = 1.0 / (1.0 + grow)
        c0 = jnp.where(live, s * (a0 * a0 + b0 * b0) + offset, -1e4)
        coef = jnp.concatenate(
            [
                c0,
                (2.0 * s) * (a0 * a1 + b0 * b1),
                (2.0 * s) * (a0 * a2 + b0 * b2),
                s * (a1 * a1 + b1 * b1),
                (2.0 * s) * (a1 * a2 + b1 * b2),
                s * (a2 * a2 + b2 * b2),
                zero1,
                zero1,
            ],
            axis=0,
        )
        coef = jnp.concatenate([p.astype(F32) for p in split3(coef)] + [zero8], axis=0).astype(BF16)
        alpha = jnp.exp2(dot_nn(mono_col[:, 0:32], coef))
        logkeep = jnp.log(1.0 - alpha)
        trans = jnp.exp(dot_nn(jnp.concatenate(split2(logkeep), axis=1), before[...]))
        w = alpha * trans
        wh, wl = split2(w)
        w2 = jnp.concatenate([wh, wl], axis=1)
        am = dot_nn(w2, sign[...])
        bm = dot_nn(jnp.concatenate(split2(w * depth), axis=1), sign[...])

        vh, vl = split2(v8)
        v16 = jnp.concatenate([vh.astype(F32), vl.astype(F32)], axis=0).astype(BF16)
        shown = dot_nt(jnp.concatenate([v16, v16], axis=1), w2)
        shown = shown[0:8] + shown[8:16]
        resid = shown[3:6] - color_ref[:, t, :]
        x8 = jnp.concatenate([normal_ref[:, t, :], resid, zero1 + 1.0, zero1], axis=0)
        y8 = v8 * y_scale + y_const
        xh, xl = [p.astype(F32) for p in split2(x8)]
        yh, yl = [p.astype(F32) for p in split2(y8)]
        x32 = jnp.concatenate([xh, xl, xh, zero8], axis=0).astype(BF16)
        y32 = jnp.concatenate([yh, yh, yl, zero8], axis=0).astype(BF16)
        grad_w = dot_tn(x32, y32) + (depth * am - bm)
        y = grad_w * w
        behind = dot_nn(jnp.concatenate(split2(y), axis=1), after[...])
        hgrad = y - behind * (alpha * jnp.exp(-logkeep))

        moments = dot_nn(mono_row[...], jnp.concatenate(split2(hgrad), axis=0))
        x16 = x32[0:16]
        dv = dot_nn(jnp.concatenate([x16, x16], axis=1), jnp.concatenate([wh, wl], axis=0))
        dv = dv[0:8] + dv[8:16]
        ga = jnp.sum(w * am, axis=0, keepdims=True)
        m0, m1, m2, m3, m4, m5 = [moments[r : r + 1] * (-kappa) for r in range(6)]

        out = jnp.concatenate(
            [
                a0 * m0 + a1 * m1 + a2 * m2,
                a0 * m1 + a1 * m3 + a2 * m4,
                a0 * m2 + a1 * m4 + a2 * m5,
                b0 * m0 + b1 * m1 + b2 * m2,
                b0 * m1 + b1 * m3 + b2 * m4,
                b0 * m2 + b1 * m4 + b2 * m5,
                (sig - 1.0) * m0,
                kappa * ga,
                dv * jnp.where(row8 < 3, -0.25 * kappa, jnp.where(row8 < 6, kappa, 0.0)),
            ],
            axis=0,
        )
        color_sum = jnp.sum(resid * resid)
        slot_sum = jnp.sum(
            2.0 * (depth * ga)
            + 0.5 * (dv[6:7] - v8[0:1] * dv[0:1] - v8[1:2] * dv[1:2] - v8[2:3] * dv[2:3])
        )
        loss_ref[pl.ds(t, 1), :] = jnp.full((1, 128), (color_sum + slot_sum) * (1.0 / 256.0), F32)

        oh, ol = [p.astype(F32) for p in split2(out)]
        both = jnp.concatenate([oh, ol], axis=1)
        high2 = jnp.concatenate([high, high], axis=1)
        spread = jnp.concatenate(
            [jnp.where(high2 == h, both, 0.0).astype(BF16) for h in range(32)], axis=0
        )
        acc[...] += dot_nt(spread, jnp.concatenate([hot, hot], axis=1))
        return c

    lax.fori_loop(0, TILES, tile, 0)
    for q in range(32):
        for half in range(2):
            pack_pair(
                acc[q * 16 : q * 16 + 16, half * 128 : half * 128 + 128], out_ref, 4 * q + 2 * half
            )


def surfel_kernel(
    back_ref, got_ref, position_ref, harmonics_ref, cams_ref, gs_ref, gp_ref, gh_ref, acc
):
    acc[...] = jnp.zeros_like(acc)

    def add(q, c):
        index = fetch_index(got_ref, q)
        hot = one_hot_rows(256, index & 255)
        high = index >> 8
        d = jnp.concatenate([unpack_pair(back_ref, 4 * q), unpack_pair(back_ref, 4 * q + 2)], axis=1)
        dh, dl = [p.astype(F32) for p in split2(d)]
        both = jnp.concatenate([dh, dl], axis=1)
        high2 = jnp.concatenate([high, high], axis=1)
        spread = jnp.concatenate(
            [jnp.where(high2 == h, both, 0.0).astype(BF16) for h in range(16)], axis=0
        )
        acc[q // 8] += dot_nt(spread, jnp.concatenate([hot, hot], axis=1))
        return c

    lax.fori_loop(0, 32, add, 0)
    cams = cams_ref[...]

    def finish(h, c):
        lanes = pl.ds(pl.multiple_of(h * 256, 256), 256)
        views = [acc[v, pl.ds(pl.multiple_of(h * 16, 16), 16), :] for v in range(4)]
        total = (views[0] + views[1]) + (views[2] + views[3])
        gs_ref[:, lanes] = total[0:11]
        dirs, length = directions([position_ref[d : d + 1, lanes] for d in range(3)], cams)
        x, y, z = dirs
        basis = sh_basis(x, y, z)
        dbasis = [jnp.zeros_like(x) for _ in range(16)]
        for ch in range(3):
            coeffs = [harmonics_ref[ch * 16 + b : ch * 16 + b + 1, lanes] for b in range(16)]
            value = jnp.zeros_like(x)
            for b in range(16):
                value = value + coeffs[b] * basis[b]
            value = value + 0.5
            dcol = jnp.concatenate([views[v][11 + ch : 12 + ch] for v in range(4)], axis=0)
            dcol = dcol * jnp.where(value > 0.0, 1.0, jnp.where(value == 0.0, 0.5, 0.0))
            for b in range(16):
                gh_ref[ch * 16 + b : ch * 16 + b + 1, lanes] = jnp.sum(
                    dcol * basis[b], axis=0, keepdims=True
                )
                dbasis[b] = dbasis[b] + dcol * coeffs[b]
        grads = sh_basis_back(x, y, z, dbasis)
        along = grads[0] * x + grads[1] * y + grads[2] * z
        for d in range(3):
            gp_ref[d : d + 1, lanes] = jnp.sum(
                (grads[d] - dirs[d] * along) / length, axis=0, keepdims=True
            )
        return c

    lax.fori_loop(0, 16, finish, 0)


VM = pl.BlockSpec(memory_space=pltpu.VMEM)
SM = pl.BlockSpec(memory_space=pltpu.SMEM)
LIMIT = 48 * 1024 * 1024


def exchange(x, collective_id, name):
    return pl.pallas_call(
        exchange_kernel,
        out_shape=jax.ShapeDtypeStruct(x.shape, x.dtype),
        in_specs=[VM],
        out_specs=VM,
        scratch_shapes=[pltpu.SemaphoreType.DMA] * 3,
        compiler_params=pltpu.CompilerParams(collective_id=collective_id, has_side_effects=True),
        name=name,
    )(x)


def local_call(kernel, out_shape, in_specs, scratch, name):
    outs = tuple(jax.ShapeDtypeStruct(s, d) for s, d in out_shape)
    return pl.pallas_call(
        kernel,
        out_shape=outs,
        in_specs=in_specs,
        out_specs=tuple(VM for _ in outs),
        scratch_shapes=scratch,
        compiler_params=pltpu.CompilerParams(vmem_limit_bytes=LIMIT),
        name=name,
    )


def on_device(
    splat, position, harmonics, cameras, tile_lists, tile_counts, target_color, target_normal
):
    send, pos = local_call(
        route_kernel,
        [((N_DEV, 1, 128), I32), ((TILES, 256), I32)],
        [VM, SM],
        [pltpu.VMEM((256, 256), BF16)],
        "route",
    )(tile_lists, tile_counts)
    got = exchange(send, 0, "exchange_requests")
    (rows,) = local_call(
        gather_kernel,
        [((N_DEV, 8, 128), F32)],
        [VM] * 5,
        [pltpu.VMEM((4, 256, 768), BF16)],
        "gather_rows",
    )(splat, position, harmonics, cameras, got)
    recv = exchange(rows, 1, "exchange_rows")
    loss, grads = local_call(
        tiles_kernel,
        [((TILES, 128), F32), ((N_DEV, 8, 128), F32)],
        [VM, VM, SM, VM, VM],
        [
            pltpu.VMEM((512, 768), BF16),
            pltpu.VMEM((512, 256), F32),
            pltpu.VMEM((512, 256), BF16),
            pltpu.VMEM((512, 256), BF16),
            pltpu.VMEM((512, 256), BF16),
            pltpu.VMEM((256, 128), BF16),
            pltpu.VMEM((16, 512), BF16),
        ],
        "composite_tiles",
    )(recv, pos, tile_counts, target_color, target_normal)
    back = exchange(grads, 1, "exchange_grads")
    gs, gp, gh = local_call(
        surfel_kernel,
        [((11, SURF), F32), ((3, SURF), F32), ((48, SURF), F32)],
        [VM] * 5,
        [pltpu.VMEM((4, 256, 256), F32)],
        "surfel_grads",
    )(back, got, position, harmonics, cameras)
    return gs, gp, gh, loss[:, 0]


def solution(mesh):
    return jax.shard_map(
        on_device,
        mesh=mesh,
        in_specs=(
            P(None, "surf"),
            P(None, "surf"),
            P(None, "surf"),
            P(),
            P("surf", None),
            P("surf"),
            P(None, "surf", None),
            P(None, "surf", None),
        ),
        out_specs=(P(None, "surf"), P(None, "surf"), P(None, "surf"), P("surf")),
        check_vma=False,
    )
```

```python
import functools

import jax
import jax.numpy as jnp
from jax import lax
from jax.experimental import pallas as pl
from jax.experimental.pallas import tpu as pltpu
from jax.sharding import PartitionSpec as P

F32 = jnp.float32
BF16 = jnp.bfloat16
I32 = jnp.int32
MESH = pl.DeviceIdType.MESH
N_DEV = 128
TILES = 32
SURF = 4096
SHARE = 48
LOG2E = 1.4426950408889634
LOG2_TOP = -0.07400058144377693
GROUP = 4

sh_zero = 0.28209479177387814
sh_one = 0.4886025119029199
sh_two = (
    1.0925484305920792,
    -1.0925484305920792,
    0.31539156525252005,
    -1.0925484305920792,
    0.5462742152960396,
)
sh_three = (
    -0.5900435899266435,
    2.890611442640554,
    -0.4570457994644658,
    0.3731763325901154,
    -0.4570457994644658,
    1.445305721320277,
    -0.5900435899266435,
)


def iota(shape, dim):
    return lax.broadcasted_iota(I32, shape, dim)


def dot_nn(a, b):
    return lax.dot_general(a, b, (((1,), (0,)), ((), ())), preferred_element_type=F32)


def dot_nt(a, b):
    return lax.dot_general(a, b, (((1,), (1,)), ((), ())), preferred_element_type=F32)


def dot_tn(a, b):
    return lax.dot_general(a, b, (((0,), (0,)), ((), ())), preferred_element_type=F32)


def split2(x):
    hi = x.astype(BF16)
    return hi, (x - hi.astype(F32)).astype(BF16)


def split3(x):
    hi = x.astype(BF16)
    rest = x - hi.astype(F32)
    mid = rest.astype(BF16)
    return hi, mid, (rest - mid.astype(F32)).astype(BF16)


def one_hot_rows(rows, index):
    return jnp.where(iota((rows, index.shape[1]), 0) == index, 1.0, 0.0).astype(BF16)


def directions(pos_rows, cams):
    offs = [pos_rows[d] - cams[:, d : d + 1] for d in range(3)]
    length = jnp.sqrt(offs[0] * offs[0] + offs[1] * offs[1] + offs[2] * offs[2])
    return [o / length for o in offs], length


def sh_basis(x, y, z):
    xx, yy, zz = x * x, y * y, z * z
    t, h = sh_two, sh_three
    return [
        jnp.full_like(x, sh_zero),
        -sh_one * y,
        sh_one * z,
        -sh_one * x,
        t[0] * (x * y),
        t[1] * (y * z),
        t[2] * (2.0 * zz - xx - yy),
        t[3] * (x * z),
        t[4] * (xx - yy),
        h[0] * (y * (3.0 * xx - yy)),
        h[1] * (x * y * z),
        h[2] * (y * (4.0 * zz - xx - yy)),
        h[3] * (z * (2.0 * zz - 3.0 * xx - 3.0 * yy)),
        h[4] * (x * (4.0 * zz - xx - yy)),
        h[5] * (z * (xx - yy)),
        h[6] * (x * (xx - 3.0 * yy)),
    ]


def sh_basis_back(x, y, z, d):
    xx, yy, zz = x * x, y * y, z * z
    xy, yz, xz = x * y, y * z, x * z
    t, h = sh_two, sh_three
    gx = (
        -sh_one * d[3] + t[0] * (y * d[4]) - (2.0 * t[2]) * (x * d[6]) + t[3] * (z * d[7])
        + (2.0 * t[4]) * (x * d[8]) + (6.0 * h[0]) * (xy * d[9]) + h[1] * (yz * d[10])
        - (2.0 * h[2]) * (xy * d[11]) - (6.0 * h[3]) * (xz * d[12])
        + h[4] * ((4.0 * zz - 3.0 * xx - yy) * d[13]) + (2.0 * h[5]) * (xz * d[14])
        + (3.0 * h[6]) * ((xx - yy) * d[15])
    )
    gy = (
        -sh_one * d[1] + t[0] * (x * d[4]) + t[1] * (z * d[5]) - (2.0 * t[2]) * (y * d[6])
        - (2.0 * t[4]) * (y * d[8]) + (3.0 * h[0]) * ((xx - yy) * d[9]) + h[1] * (xz * d[10])
        + h[2] * ((4.0 * zz - xx - 3.0 * yy) * d[11]) - (6.0 * h[3]) * (yz * d[12])
        - (2.0 * h[4]) * (xy * d[13]) - (2.0 * h[5]) * (yz * d[14]) - (6.0 * h[6]) * (xy * d[15])
    )
    gz = (
        sh_one * d[2] + t[1] * (y * d[5]) + (4.0 * t[2]) * (z * d[6]) + t[3] * (x * d[7])
        + h[1] * (xy * d[10]) + (8.0 * h[2]) * (yz * d[11])
        + h[3] * ((6.0 * zz - 3.0 * xx - 3.0 * yy) * d[12]) + (8.0 * h[4]) * (xz * d[13])
        + h[5] * ((xx - yy) * d[14])
    )
    return gx, gy, gz


def lane_of(x):
    return iota(x.shape, 1)


def join_eight(pieces):
    blocks = [jnp.zeros_like(pieces[0]) for _ in range(3)]
    for s, piece in enumerate(pieces):
        b, lo = divmod(SHARE * s, 128)
        lane = lane_of(piece)
        blocks[b] = jnp.where((lane >= lo) & (lane < lo + SHARE), piece, blocks[b])
        if lo + SHARE > 128:
            blocks[b + 1] = jnp.where(lane < lo + SHARE - 128, piece, blocks[b + 1])
    return blocks


def split_eight(blocks):
    pieces = []
    for s in range(8):
        b, lo = divmod(SHARE * s, 128)
        piece = pltpu.roll(blocks[b], 128 - lo, 1) if lo else blocks[b]
        if lo + SHARE > 128:
            piece = jnp.where(
                lane_of(piece) < 128 - lo, piece, pltpu.roll(blocks[b + 1], 128 - lo, 1)
            )
        pieces.append(piece)
    return pieces


def shift(x, amount):
    return pltpu.roll(x, amount % 128, 1) if amount % 128 else x


def index_blocks(ref, first):
    return join_eight([shift(ref[first + s], SHARE * s) for s in range(8)])


def message_blocks(ref, first):
    pieces = []
    for s in range(8):
        tile = ref[first + s]
        pieces.append(
            jnp.concatenate([shift(tile, SHARE * s), shift(tile, SHARE * s + 64)], axis=0)
        )
    return join_eight(pieces)


def write_messages(ref, first, blocks):
    for s, piece in enumerate(split_eight(blocks)):
        ref[first + s] = jnp.where(
            lane_of(piece[0:8]) < 64, piece[0:8], pltpu.roll(piece[8:16], 64, 1)
        )


def wide(blocks):
    return [
        jnp.concatenate(blocks[2 * i : 2 * i + 2], axis=1) for i in range(len(blocks) // 2)
    ]


def halves(chunks):
    return [c[:, 128 * i : 128 * i + 128] for c in chunks for i in range(2)]


def pick_rows(found, high, count):
    parts = [jnp.where(high == h, found[h * 16 : h * 16 + 16], 0.0) for h in range(count)]
    while len(parts) > 1:
        pairs = [parts[i] + parts[i + 1] for i in range(0, len(parts) - 1, 2)]
        parts = pairs + ([parts[-1]] if len(parts) % 2 else [])
    return parts[0]


def look_up(table, index, count, splits):
    hot = one_hot_rows(256, index & 255)
    found = dot_nn(table, jnp.concatenate([hot] * splits, axis=0))
    return pick_rows(found, index >> 8, count)


def route(lists_ref, counts_ref, send_ref, slot_ref, pos_ref, upper):
    upper[...] = jnp.where(iota((256, 256), 0) < iota((256, 256), 1), 1.0, 0.0).astype(BF16)
    holder_id = iota((N_DEV, 256), 0)
    lane = iota((1, 256), 1)
    rank_id = iota((N_DEV, 256), 0) & 63
    group = 4

    def tiles(i, state):
        carry, sums = state
        hots, ranks = [], []
        ones = []
        flats = [lists_ref[pl.ds(i * group + u, 1), :] for u in range(group)]
        lives = [lane < counts_ref[i * group + u] for u in range(group)]
        holders = [jnp.where(lives[u], flats[u] // SURF, -1) for u in range(group)]
        ones = [jnp.where(holder_id == h, 1.0, 0.0) for h in holders]
        counts = dot_nn(jnp.concatenate(ones, axis=0).astype(BF16), upper[...])
        left, right = [], []
        for u in range(group):
            count = counts[u * N_DEV : u * N_DEV + N_DEV] + carry
            rank = jnp.sum(ones[u] * count, axis=0, keepdims=True).astype(I32)
            carry = carry + jnp.sum(ones[u], axis=1, keepdims=True)
            pos_ref[pl.ds(i * group + u, 1), :] = jnp.where(
                lives[u], holders[u] * SHARE + rank, -1
            )
            local = flats[u] % SURF
            values = [
                (local // 64).astype(F32),
                (local % 64).astype(F32),
                lane.astype(F32),
                jnp.full((1, 256), i * group + u, I32).astype(F32),
            ]
            left.append(jnp.concatenate([ones[u] * v for v in values], axis=0).astype(BF16))
            right.append(jnp.where(rank_id == rank, 1.0, 0.0).astype(BF16))
        sums = sums + dot_nt(jnp.concatenate(left, axis=1), jnp.concatenate(right, axis=1))
        return carry, sums

    _, sums = lax.fori_loop(
        0, TILES // group, tiles, (jnp.zeros((N_DEV, 1), F32), jnp.zeros((4 * N_DEV, 128), F32))
    )
    named = (iota((N_DEV, 128), 1) & 63) < SHARE
    local = (sums[0:128] * 64.0 + sums[128:256]).astype(I32)
    slot = (sums[384:512] * 256.0 + sums[256:384]).astype(I32)
    send_ref[:, 0, :] = jnp.where(named, local, -1)
    slot_ref[:, 0, :] = jnp.where(named, slot, -1)


def build_rows(splat_ref, position_ref, harmonics_ref, cams_ref, table):
    cams = cams_ref[...]

    def build(h, c):
        lanes = pl.ds(pl.multiple_of(h * 256, 256), 256)
        (x, y, z), _ = directions([position_ref[d : d + 1, lanes] for d in range(3)], cams)
        basis = sh_basis(x, y, z)
        colors = []
        for ch in range(3):
            total = jnp.zeros_like(x)
            for b in range(16):
                total = total + harmonics_ref[ch * 16 + b : ch * 16 + b + 1, lanes] * basis[b]
            colors.append(jnp.maximum(total + 0.5, 0.0))
        splat = splat_ref[:, lanes]
        for v in range(4):
            rows = jnp.concatenate(
                [splat] + [col[v : v + 1] for col in colors] + [jnp.zeros((2, 256), F32)], axis=0
            )
            table[v, pl.ds(pl.multiple_of(h * 16, 16), 16), :] = jnp.concatenate(split3(rows), axis=1)
        return c

    lax.fori_loop(0, 16, build, 0)


def fetch_rows(step, got_ref, out_ref, table):
    index = index_blocks(got_ref, step * 16) + index_blocks(got_ref, step * 16 + 8)
    found = halves([look_up(table[step // 2], i, 16, 3) for i in wide(index)])
    write_messages(out_ref, step * 16, found[0:3])
    write_messages(out_ref, step * 16 + 8, found[3:6])


def monomials(pixel, which):
    px = ((pixel & 15).astype(F32) - 7.5) * 0.125
    py = ((pixel >> 4).astype(F32) - 7.5) * 0.125
    m = jnp.where(which == 0, 1.0, 0.0)
    for n, value in ((1, px), (2, py), (3, px * px), (4, px * py), (5, py * py)):
        m = jnp.where(which == n, value, m)
    return m


def stack(parts):
    return jnp.concatenate(parts, axis=0)


def beside(parts):
    return jnp.concatenate(parts, axis=1)


def unstack(x, rows, count):
    return [x[rows * i : rows * i + rows] for i in range(count)]


def arrange_rows(recv_ref, table):
    def unpack(step, c):
        blocks = message_blocks(recv_ref, step * 16) + message_blocks(recv_ref, step * 16 + 8)
        for n, g in enumerate(wide(blocks)):
            table[pl.ds(pl.multiple_of(step * 48 + n * 16, 16), 16), :] = beside(split2(g))
        return c

    lax.fori_loop(0, 8, unpack, 0)


def composite(
    pos_ref, counts_ref, color_ref, normal_ref, loss_ref, table, grads, before, sign, after, mono_col
):
    j, k = iota((512, 256), 0) & 255, iota((512, 256), 1)
    before[...] = jnp.where(j < k, 1.0, 0.0).astype(BF16)
    sign[...] = jnp.where(j < k, 1.0, jnp.where(j > k, -1.0, 0.0)).astype(BF16)
    after[...] = jnp.where(j > k, 1.0, 0.0).astype(BF16)
    col = iota((256, 128), 1)
    mono_col[...] = jnp.where(col < 24, monomials(iota((256, 128), 0), col & 7), 0.0).astype(BF16)

    lane = iota((1, 256), 1)
    row8 = iota((8, 256), 0)
    y_scale = jnp.where(row8 < 3, -0.25, jnp.where(row8 < 6, 1.0, 0.0))
    y_const = jnp.where(row8 == 6, 0.25, 0.0)
    kappa = 2.0 / 256.0
    dv_scale = jnp.where(row8 < 3, -0.25 * kappa, jnp.where(row8 < 6, kappa, 0.0))
    px_low = (row8.astype(F32) - 7.5) * 0.125
    px_high = px_low + 1.0
    zero1 = jnp.zeros((1, 256), F32)
    zero8 = jnp.zeros((8, 256), F32)

    def tiles(i, c):
        ts = [i * GROUP + u for u in range(GROUP)]
        each = range(GROUP)
        rows = []
        for t in ts:
            rows.append(look_up(table[...], pos_ref[pl.ds(t, 1), :], 24, 2))
        coefs, sigs = [], []
        for u, t in enumerate(ts):
            a0, a1, a2, b0, b1, b2, logit = [rows[u][r : r + 1] for r in range(7)]
            s = -0.5 * LOG2E
            grow = jnp.exp(-logit)
            offset = jnp.log(1.0 + grow) * (-LOG2E) + LOG2_TOP
            sigs.append(1.0 / (1.0 + grow))
            c0 = jnp.where(lane < counts_ref[t], s * (a0 * a0 + b0 * b0) + offset, -1e4)
            coef = stack(
                [
                    c0,
                    (2.0 * s) * (a0 * a1 + b0 * b1),
                    (2.0 * s) * (a0 * a2 + b0 * b2),
                    s * (a1 * a1 + b1 * b1),
                    (2.0 * s) * (a1 * a2 + b1 * b2),
                    s * (a2 * a2 + b2 * b2),
                    zero1,
                    zero1,
                ]
            )
            coefs.append(stack([p.astype(F32) for p in split3(coef)] + [zero8]).astype(BF16))
        depth = [rows[u][7:8] for u in each]
        v8 = [rows[u][8:16] for u in each]
        alpha = [jnp.exp2(dot_nn(mono_col[:, 0:32], coefs[u])) for u in each]
        logkeep = [jnp.log(1.0 - alpha[u]) for u in each]
        seen = unstack(
            dot_nn(stack([beside(split2(logkeep[u])) for u in each]), before[...]), 256, GROUP
        )
        w = [alpha[u] * jnp.exp(seen[u]) for u in each]
        w2 = [beside(split2(w[u])) for u in each]
        sums = unstack(
            dot_nn(stack(w2 + [beside(split2(w[u] * depth[u])) for u in each]), sign[...]),
            256,
            2 * GROUP,
        )
        am, bm = sums[0:GROUP], sums[GROUP:]
        resid, x32, y = [], [], []
        for u, t in enumerate(ts):
            v16 = stack([p.astype(F32) for p in split2(v8[u])]).astype(BF16)
            shown = dot_nt(beside([v16, v16]), w2[u])
            shown = shown[0:8] + shown[8:16]
            resid.append(shown[3:6] - color_ref[:, t, :])
        for u, t in enumerate(ts):
            x8 = stack([normal_ref[:, t, :], resid[u], zero1 + 1.0, zero1])
            xh, xl = [p.astype(F32) for p in split2(x8)]
            yh, yl = [p.astype(F32) for p in split2(v8[u] * y_scale + y_const)]
            x32.append(stack([xh, xl, xh, zero8]).astype(BF16))
            y32 = stack([yh, yh, yl, zero8]).astype(BF16)
            y.append((dot_tn(x32[u], y32) + (depth[u] * am[u] - bm[u])) * w[u])
        behind = unstack(
            dot_nn(stack([beside(split2(y[u])) for u in each]), after[...]), 256, GROUP
        )
        for u, t in enumerate(ts):
            hgrad = y[u] - behind[u] * (alpha[u] * jnp.exp(-logkeep[u]))
            low = [zero8] * 3
            high = [zero8] * 3
            for r in range(16):
                low[0] = low[0] + hgrad[r * 16 : r * 16 + 8]
                high[0] = high[0] + hgrad[r * 16 + 8 : r * 16 + 16]
                for n in (1, 2):
                    low[n] = low[n] + low[n - 1]
                    high[n] = high[n] + high[n - 1]

            def moment(first, second):
                return jnp.sum(first + second, axis=0, keepdims=True) * (-kappa)

            def rows_of(f):
                return f[0], 1.0625 * f[0] - 0.125 * f[1], (
                    1.12890625 * f[0] - 0.28125 * f[1] + 0.03125 * f[2]
                )

            low, high = rows_of(low), rows_of(high)
            m0 = moment(low[0], high[0])
            m1 = moment(low[0] * px_low, high[0] * px_high)
            m2 = moment(low[1], high[1])
            m3 = moment(low[0] * (px_low * px_low), high[0] * (px_high * px_high))
            m4 = moment(low[1] * px_low, high[1] * px_high)
            m5 = moment(low[2], high[2])
            x16 = x32[u][0:16]
            dv = dot_nn(beside([x16, x16]), stack([w2[u][:, 0:256], w2[u][:, 256:512]]))
            dv = dv[0:8] + dv[8:16]
            ga = jnp.sum(w[u] * am[u], axis=0, keepdims=True)
            a0, a1, a2, b0, b1, b2 = [rows[u][r : r + 1] for r in range(6)]
            out = stack(
                [
                    a0 * m0 + a1 * m1 + a2 * m2,
                    a0 * m1 + a1 * m3 + a2 * m4,
                    a0 * m2 + a1 * m4 + a2 * m5,
                    b0 * m0 + b1 * m1 + b2 * m2,
                    b0 * m1 + b1 * m3 + b2 * m4,
                    b0 * m2 + b1 * m4 + b2 * m5,
                    (sigs[u] - 1.0) * m0,
                    kappa * ga,
                    dv * dv_scale,
                ]
            )
            grads[pl.ds(pl.multiple_of(t * 16, 16), 16), :] = beside(split2(out))
            facing = v8[u][0:3] * dv[0:3]
            loss = (
                jnp.sum(resid[u] * resid[u] - 0.5 * facing, axis=0, keepdims=True)
                + 2.0 * (depth[u] * ga)
                + 0.5 * dv[6:7]
            ) * (1.0 / 256.0)
            loss_ref[pl.ds(t, 1), :] = loss[:, 0:128] + loss[:, 128:256]
        return c

    lax.fori_loop(0, TILES // GROUP, tiles, 0)


def return_rows(step, slot_ref, out_ref, grads):
    index = index_blocks(slot_ref, step * 16) + index_blocks(slot_ref, step * 16 + 8)
    found = halves([look_up(grads[...], i, 32, 2) for i in wide(index)])
    write_messages(out_ref, step * 16, found[0:3])
    write_messages(out_ref, step * 16 + 8, found[3:6])


def sum_rows(step, back_ref, got_ref, acc):
    index = wide(index_blocks(got_ref, step * 16) + index_blocks(got_ref, step * 16 + 8))
    data = wide(message_blocks(back_ref, step * 16) + message_blocks(back_ref, step * 16 + 8))
    left, right = [], []
    for i, d in zip(index, data):
        hot = one_hot_rows(256, i & 255)
        both = beside([p.astype(F32) for p in split2(d)])
        high = beside([i >> 8, i >> 8])
        left.append(stack([jnp.where(high == h, both, 0.0).astype(BF16) for h in range(16)]))
        right += [hot, hot]
    acc[step // 2] += dot_nt(beside(left), beside(right))


def finish_grads(position_ref, harmonics_ref, cams_ref, gs_ref, gp_ref, gh_ref, acc):
    cams = cams_ref[...]

    def finish(h, c):
        lanes = pl.ds(pl.multiple_of(h * 256, 256), 256)
        views = [acc[v, pl.ds(pl.multiple_of(h * 16, 16), 16), :] for v in range(4)]
        total = (views[0] + views[1]) + (views[2] + views[3])
        gs_ref[:, lanes] = total[0:11]
        dirs, length = directions([position_ref[d : d + 1, lanes] for d in range(3)], cams)
        x, y, z = dirs
        basis = sh_basis(x, y, z)
        dbasis = [jnp.zeros_like(x) for _ in range(16)]
        for ch in range(3):
            coeffs = [harmonics_ref[ch * 16 + b : ch * 16 + b + 1, lanes] for b in range(16)]
            value = jnp.zeros_like(x)
            for b in range(16):
                value = value + coeffs[b] * basis[b]
            value = value + 0.5
            dcol = stack([views[v][11 + ch : 12 + ch] for v in range(4)])
            dcol = dcol * jnp.where(value > 0.0, 1.0, jnp.where(value == 0.0, 0.5, 0.0))
            for b in range(16):
                gh_ref[ch * 16 + b : ch * 16 + b + 1, lanes] = jnp.sum(
                    dcol * basis[b], axis=0, keepdims=True
                )
                dbasis[b] = dbasis[b] + dcol * coeffs[b]
        grads = sh_basis_back(x, y, z, dbasis)
        along = grads[0] * x + grads[1] * y + grads[2] * z
        for d in range(3):
            gp_ref[d : d + 1, lanes] = jnp.sum(
                (grads[d] - dirs[d] * along) / length, axis=0, keepdims=True
            )
        return c

    lax.fori_loop(0, 16, finish, 0)


def greet_all(me):
    barrier = pltpu.get_barrier_semaphore()

    def greet(i, c):
        pl.semaphore_signal(
            barrier, inc=1, device_id=(lax.rem(me + i, N_DEV),), device_id_type=MESH
        )
        return c

    lax.fori_loop(1, N_DEV, greet, 0)


def send_block(src_ref, dst_ref, me, peer, send_sem, recv_sem):
    pltpu.make_async_remote_copy(
        src_ref=src_ref.at[peer],
        dst_ref=dst_ref.at[me],
        send_sem=send_sem,
        recv_sem=recv_sem,
        device_id=(peer,),
        device_id_type=MESH,
    ).start()


def wait_all(src_ref, dst_ref, me, send_sem, recv_sem):
    pltpu.make_async_remote_copy(
        src_ref=src_ref.at[pl.ds(0, N_DEV - 1)],
        dst_ref=dst_ref.at[pl.ds(0, N_DEV - 1)],
        send_sem=send_sem,
        recv_sem=recv_sem,
        device_id=(me,),
        device_id_type=MESH,
    ).wait()


def make_and_send(make, src_ref, dst_ref, me, send_sem, recv_sem):
    def steps(i, c):
        step = lax.rem(me // 16 + i, 8)
        make(step)

        def send(s, d):
            peer = step * 16 + s

            @pl.when(peer != me)
            def _():
                send_block(src_ref, dst_ref, me, peer, send_sem, recv_sem)

            return d

        lax.fori_loop(0, 16, send, 0)
        return c

    lax.fori_loop(0, 8, steps, 0)
    dst_ref[me] = src_ref[me]
    wait_all(src_ref, dst_ref, me, send_sem, recv_sem)


def step_kernel(
    splat_ref, position_ref, harmonics_ref, cams_ref, lists_ref, counts_ref, color_ref, normal_ref,
    gs_ref, gp_ref, gh_ref, loss_ref,
    ask, got, slot, pos, rows, recv, grad_rows, back, upper, surfels, table, grads, acc,
    before, sign, after, mono_col, send_sem, recv_sem,
):
    me = lax.axis_index("surf")
    greet_all(me)
    route(lists_ref, counts_ref, ask, slot, pos, upper)
    pl.semaphore_wait(pltpu.get_barrier_semaphore(), N_DEV - 1)

    def request(i, c):
        send_block(ask, got, me, lax.rem(me + i, N_DEV), send_sem.at[0], recv_sem.at[0])
        return c

    lax.fori_loop(1, N_DEV, request, 0)
    got[me] = ask[me]
    build_rows(splat_ref, position_ref, harmonics_ref, cams_ref, surfels)
    wait_all(ask, got, me, send_sem.at[0], recv_sem.at[0])
    make_and_send(
        lambda step: fetch_rows(step, got, rows, surfels),
        rows, recv, me, send_sem.at[1], recv_sem.at[1],
    )
    arrange_rows(recv, table)
    composite(
        pos, counts_ref, color_ref, normal_ref, loss_ref, table, grads, before, sign, after, mono_col
    )
    make_and_send(
        lambda step: return_rows(step, slot, grad_rows, grads),
        grad_rows, back, me, send_sem.at[2], recv_sem.at[2],
    )
    acc[...] = jnp.zeros_like(acc)

    def add(step, c):
        sum_rows(step, back, got, acc)
        return c

    lax.fori_loop(0, 8, add, 0)
    finish_grads(position_ref, harmonics_ref, cams_ref, gs_ref, gp_ref, gh_ref, acc)


VM = pl.BlockSpec(memory_space=pltpu.VMEM)
SM = pl.BlockSpec(memory_space=pltpu.SMEM)
LIMIT = 48 * 1024 * 1024


def on_device(
    splat, position, harmonics, cameras, tile_lists, tile_counts, target_color, target_normal
):
    gs, gp, gh, loss = pl.pallas_call(
        step_kernel,
        out_shape=(
            jax.ShapeDtypeStruct((11, SURF), F32),
            jax.ShapeDtypeStruct((3, SURF), F32),
            jax.ShapeDtypeStruct((48, SURF), F32),
            jax.ShapeDtypeStruct((TILES, 128), F32),
        ),
        in_specs=[VM, VM, VM, VM, VM, SM, VM, VM],
        out_specs=(VM, VM, VM, VM),
        scratch_shapes=[
            pltpu.VMEM((N_DEV, 1, 128), I32),
            pltpu.VMEM((N_DEV, 1, 128), I32),
            pltpu.VMEM((N_DEV, 1, 128), I32),
            pltpu.VMEM((TILES, 256), I32),
            pltpu.VMEM((N_DEV, 8, 128), F32),
            pltpu.VMEM((N_DEV, 8, 128), F32),
            pltpu.VMEM((N_DEV, 8, 128), F32),
            pltpu.VMEM((N_DEV, 8, 128), F32),
            pltpu.VMEM((256, 256), BF16),
            pltpu.VMEM((4, 256, 768), BF16),
            pltpu.VMEM((384, 512), BF16),
            pltpu.VMEM((512, 512), BF16),
            pltpu.VMEM((4, 256, 256), F32),
            pltpu.VMEM((512, 256), BF16),
            pltpu.VMEM((512, 256), BF16),
            pltpu.VMEM((512, 256), BF16),
            pltpu.VMEM((256, 128), BF16),
            pltpu.SemaphoreType.DMA((3,)),
            pltpu.SemaphoreType.DMA((3,)),
        ],
        compiler_params=pltpu.CompilerParams(
            collective_id=0, has_side_effects=True, vmem_limit_bytes=LIMIT
        ),
        name="surfel_step",
    )(splat, position, harmonics, cameras, tile_lists, tile_counts, target_color, target_normal)
    return gs, gp, gh, jnp.sum(loss, axis=1)


def solution(mesh):
    return jax.shard_map(
        on_device,
        mesh=mesh,
        in_specs=(
            P(None, "surf"),
            P(None, "surf"),
            P(None, "surf"),
            P(),
            P("surf", None),
            P("surf"),
            P(None, "surf", None),
            P(None, "surf", None),
        ),
        out_specs=(P(None, "surf"), P(None, "surf"), P(None, "surf"), P("surf")),
        check_vma=False,
    )
```

```python
import functools

import jax
import jax.numpy as jnp
from jax import lax
from jax.experimental import pallas as pl
from jax.experimental.pallas import tpu as pltpu
from jax.sharding import PartitionSpec as P

F32 = jnp.float32
BF16 = jnp.bfloat16
I32 = jnp.int32
MESH = pl.DeviceIdType.MESH
N_DEV = 128
TILES = 32
SURF = 4096
SHARE = 48
LOG2E = 1.4426950408889634
LOG2_TOP = -0.07400058144377693
GROUP = 8

sh_zero = 0.28209479177387814
sh_one = 0.4886025119029199
sh_two = (
    1.0925484305920792,
    -1.0925484305920792,
    0.31539156525252005,
    -1.0925484305920792,
    0.5462742152960396,
)
sh_three = (
    -0.5900435899266435,
    2.890611442640554,
    -0.4570457994644658,
    0.3731763325901154,
    -0.4570457994644658,
    1.445305721320277,
    -0.5900435899266435,
)


def iota(shape, dim):
    return lax.broadcasted_iota(I32, shape, dim)


def dot_nn(a, b):
    return lax.dot_general(a, b, (((1,), (0,)), ((), ())), preferred_element_type=F32)


def dot_nt(a, b):
    return lax.dot_general(a, b, (((1,), (1,)), ((), ())), preferred_element_type=F32)


def dot_tn(a, b):
    return lax.dot_general(a, b, (((0,), (0,)), ((), ())), preferred_element_type=F32)


def split2(x):
    hi = x.astype(BF16)
    return hi, (x - hi.astype(F32)).astype(BF16)


def split3(x):
    hi = x.astype(BF16)
    rest = x - hi.astype(F32)
    mid = rest.astype(BF16)
    return hi, mid, (rest - mid.astype(F32)).astype(BF16)


def one_hot_rows(rows, index):
    return jnp.where(iota((rows, index.shape[1]), 0) == index, 1.0, 0.0).astype(BF16)


def directions(pos_rows, cams):
    offs = [pos_rows[d] - cams[:, d : d + 1] for d in range(3)]
    length = jnp.sqrt(offs[0] * offs[0] + offs[1] * offs[1] + offs[2] * offs[2])
    return [o / length for o in offs], length


def sh_basis(x, y, z):
    xx, yy, zz = x * x, y * y, z * z
    t, h = sh_two, sh_three
    return [
        jnp.full_like(x, sh_zero),
        -sh_one * y,
        sh_one * z,
        -sh_one * x,
        t[0] * (x * y),
        t[1] * (y * z),
        t[2] * (2.0 * zz - xx - yy),
        t[3] * (x * z),
        t[4] * (xx - yy),
        h[0] * (y * (3.0 * xx - yy)),
        h[1] * (x * y * z),
        h[2] * (y * (4.0 * zz - xx - yy)),
        h[3] * (z * (2.0 * zz - 3.0 * xx - 3.0 * yy)),
        h[4] * (x * (4.0 * zz - xx - yy)),
        h[5] * (z * (xx - yy)),
        h[6] * (x * (xx - 3.0 * yy)),
    ]


def sh_basis_back(x, y, z, d):
    xx, yy, zz = x * x, y * y, z * z
    xy, yz, xz = x * y, y * z, x * z
    t, h = sh_two, sh_three
    gx = (
        -sh_one * d[3] + t[0] * (y * d[4]) - (2.0 * t[2]) * (x * d[6]) + t[3] * (z * d[7])
        + (2.0 * t[4]) * (x * d[8]) + (6.0 * h[0]) * (xy * d[9]) + h[1] * (yz * d[10])
        - (2.0 * h[2]) * (xy * d[11]) - (6.0 * h[3]) * (xz * d[12])
        + h[4] * ((4.0 * zz - 3.0 * xx - yy) * d[13]) + (2.0 * h[5]) * (xz * d[14])
        + (3.0 * h[6]) * ((xx - yy) * d[15])
    )
    gy = (
        -sh_one * d[1] + t[0] * (x * d[4]) + t[1] * (z * d[5]) - (2.0 * t[2]) * (y * d[6])
        - (2.0 * t[4]) * (y * d[8]) + (3.0 * h[0]) * ((xx - yy) * d[9]) + h[1] * (xz * d[10])
        + h[2] * ((4.0 * zz - xx - 3.0 * yy) * d[11]) - (6.0 * h[3]) * (yz * d[12])
        - (2.0 * h[4]) * (xy * d[13]) - (2.0 * h[5]) * (yz * d[14]) - (6.0 * h[6]) * (xy * d[15])
    )
    gz = (
        sh_one * d[2] + t[1] * (y * d[5]) + (4.0 * t[2]) * (z * d[6]) + t[3] * (x * d[7])
        + h[1] * (xy * d[10]) + (8.0 * h[2]) * (yz * d[11])
        + h[3] * ((6.0 * zz - 3.0 * xx - 3.0 * yy) * d[12]) + (8.0 * h[4]) * (xz * d[13])
        + h[5] * ((xx - yy) * d[14])
    )
    return gx, gy, gz


def lane_of(x):
    return iota(x.shape, 1)


def join_eight(pieces):
    blocks = [jnp.zeros_like(pieces[0]) for _ in range(3)]
    for s, piece in enumerate(pieces):
        b, lo = divmod(SHARE * s, 128)
        lane = lane_of(piece)
        blocks[b] = jnp.where((lane >= lo) & (lane < lo + SHARE), piece, blocks[b])
        if lo + SHARE > 128:
            blocks[b + 1] = jnp.where(lane < lo + SHARE - 128, piece, blocks[b + 1])
    return blocks


def split_eight(blocks):
    pieces = []
    for s in range(8):
        b, lo = divmod(SHARE * s, 128)
        piece = pltpu.roll(blocks[b], 128 - lo, 1) if lo else blocks[b]
        if lo + SHARE > 128:
            piece = jnp.where(
                lane_of(piece) < 128 - lo, piece, pltpu.roll(blocks[b + 1], 128 - lo, 1)
            )
        pieces.append(piece)
    return pieces


def shift(x, amount):
    return pltpu.roll(x, amount % 128, 1) if amount % 128 else x


def index_blocks(ref, first):
    return join_eight([shift(ref[first + s], SHARE * s) for s in range(8)])


def message_blocks(ref, first):
    pieces = []
    for s in range(8):
        tile = ref[first + s]
        pieces.append(
            jnp.concatenate([shift(tile, SHARE * s), shift(tile, SHARE * s + 64)], axis=0)
        )
    return join_eight(pieces)


def write_messages(ref, first, blocks):
    for s, piece in enumerate(split_eight(blocks)):
        ref[first + s] = jnp.where(
            lane_of(piece[0:8]) < 64, piece[0:8], pltpu.roll(piece[8:16], 64, 1)
        )


def wide(blocks):
    return [
        jnp.concatenate(blocks[2 * i : 2 * i + 2], axis=1) for i in range(len(blocks) // 2)
    ]


def halves(chunks):
    return [c[:, 128 * i : 128 * i + 128] for c in chunks for i in range(2)]


def pick_rows(found, high, count):
    parts = [jnp.where(high == h, found[h * 16 : h * 16 + 16], 0.0) for h in range(count)]
    while len(parts) > 1:
        pairs = [parts[i] + parts[i + 1] for i in range(0, len(parts) - 1, 2)]
        parts = pairs + ([parts[-1]] if len(parts) % 2 else [])
    return parts[0]


def look_up(table, index, count, splits):
    hot = one_hot_rows(256, index & 255)
    found = dot_nn(table, jnp.concatenate([hot] * splits, axis=0))
    return pick_rows(found, index >> 8, count)


def tall(row):
    return jnp.concatenate([jnp.broadcast_to(row, (16, 256)).astype(BF16)] * (N_DEV // 16), axis=0)


def route(lists_ref, counts_ref, send_ref, slot_ref, pos_ref, upper, greet):
    col = iota((256, 384), 1)
    upper[...] = jnp.where((iota((256, 384), 0) < col) | (col > 255), 1.0, 0.0).astype(BF16)
    holder_id = iota((N_DEV, 256), 0)
    lane = iota((1, 256), 1)
    rank_id = iota((N_DEV, 256), 0) & 63
    group = 4

    def tiles(i, state):
        carry, sums = state
        greet(i)
        flats = [lists_ref[pl.ds(i * group + u, 1), :] for u in range(group)]
        lives = [lane < counts_ref[i * group + u] for u in range(group)]
        holders = [jnp.where(lives[u], flats[u] // SURF, -1) for u in range(group)]
        ones = [jnp.where(holder_id == h, 1.0, 0.0) for h in holders]
        marks = [o.astype(BF16) for o in ones]
        counts = dot_nn(jnp.concatenate(marks, axis=0), upper[...])
        left, right = [], []
        for u in range(group):
            count = counts[u * N_DEV : u * N_DEV + N_DEV]
            rank = jnp.sum(
                ones[u] * (count[:, 0:256] + beside([carry, carry])), axis=0, keepdims=True
            ).astype(I32)
            carry = carry + count[:, 256:384]
            pos_ref[pl.ds(i * group + u, 1), :] = jnp.where(
                lives[u], holders[u] * SHARE + rank, -1
            )
            local = flats[u] % SURF
            values = [
                (local // 8 - 256).astype(F32),
                (local % 8 * TILES + (i * group + u)).astype(F32),
                lane.astype(F32),
            ]
            left.append(jnp.concatenate([marks[u] * tall(v) for v in values], axis=0))
            right.append(jnp.where(rank_id == rank, 1.0, 0.0).astype(BF16))
        sums = sums + dot_nt(jnp.concatenate(left, axis=1), jnp.concatenate(right, axis=1))
        return carry, sums

    _, sums = lax.fori_loop(
        0, TILES // group, tiles, (jnp.zeros((N_DEV, 128), F32), jnp.zeros((3 * N_DEV, 128), F32))
    )
    named = (iota((N_DEV, 128), 1) & 63) < SHARE
    low = sums[128:256].astype(I32)
    local = (sums[0:128].astype(I32) + 256) * 8 + low // TILES
    slot = low % TILES * 256 + sums[256:384].astype(I32)
    send_ref[:, 0, :] = jnp.where(named, local, -1)
    slot_ref[:, 0, :] = jnp.where(named, slot, -1)


def put_row(tmp, b, value):
    for half in range(2):
        tmp[half * 128 + b * 8 : half * 128 + b * 8 + 4, :] = value[:, half * 128 : half * 128 + 128]


def row_of(tmp, b):
    return jnp.concatenate(
        [tmp[half * 128 + b * 8 : half * 128 + b * 8 + 4, :] for half in range(2)], axis=1
    )


def column(tmp, v):
    return jnp.concatenate(
        [tmp[pl.ds(half * 128 + v, 16, stride=8), :] for half in range(2)], axis=1
    )


def build_rows(
    splat_ref, position_ref, harmonics_ref, cams_ref, table, basis_ref, dirs_ref, mask_ref, tmp, request
):
    cams = cams_ref[...]

    def build(h, own):
        request(h, own)
        lanes = pl.ds(pl.multiple_of(h * 256, 256), 256)
        dirs, length = directions([position_ref[d : d + 1, lanes] for d in range(3)], cams)
        for d, value in enumerate(dirs + [1.0 / length]):
            dirs_ref[d, :, lanes] = value
        for b, value in enumerate(sh_basis(*dirs)):
            put_row(tmp, b, value)
        splat = splat_ref[:, lanes]
        coeffs = [harmonics_ref[ch * 16 : ch * 16 + 16, lanes] for ch in range(3)]
        for v in range(4):
            basis = column(tmp, v)
            basis_ref[v, :, lanes] = basis
            colors = []
            for ch in range(3):
                value = jnp.sum(coeffs[ch] * basis, axis=0, keepdims=True) + 0.5
                mask_ref[ch * 4 + v : ch * 4 + v + 1, lanes] = jnp.where(
                    value > 0.0, 1.0, jnp.where(value == 0.0, 0.5, 0.0)
                )
                colors.append(jnp.maximum(value, 0.0))
            rows = jnp.concatenate([splat] + colors + [jnp.zeros((2, 256), F32)], axis=0)
            table[v, pl.ds(pl.multiple_of(h * 16, 16), 16), :] = jnp.concatenate(split2(rows), axis=1)

    for i in range(4):
        lax.fori_loop(4 * i, 4 * i + 4, lambda h, c: build(h, i) or c, 0)


def plane_blocks(blocks_of_eight, ref, plane):
    return wide([b for s in range(4) for b in blocks_of_eight(ref, plane * 32 + s * 8)])


def write_plane(ref, plane, index, count, table, between):
    chunks = []
    for n, i in enumerate(index):
        chunks.append(look_up(table, i, count, 2))
        between(n)
    blocks = halves(chunks)
    for s in range(4):
        write_messages(ref, plane * 32 + s * 8, blocks[3 * s : 3 * s + 3])


def fetch_rows(plane, got_ref, out_ref, table, between):
    index = plane_blocks(index_blocks, got_ref, plane)
    write_plane(out_ref, plane, index, 16, table[plane], between)


def monomials(pixel, which):
    px = ((pixel & 15).astype(F32) - 7.5) * 0.125
    py = ((pixel >> 4).astype(F32) - 7.5) * 0.125
    m = jnp.where(which == 0, 1.0, 0.0)
    for n, value in ((1, px), (2, py), (3, px * px), (4, px * py), (5, py * py)):
        m = jnp.where(which == n, value, m)
    return m


def stack(parts):
    return jnp.concatenate(parts, axis=0)


def beside(parts):
    return jnp.concatenate(parts, axis=1)


def unstack(x, rows, count):
    return [x[rows * i : rows * i + rows] for i in range(count)]


def arrange_rows(plane, recv_ref, table):
    for n, g in enumerate(plane_blocks(message_blocks, recv_ref, plane)):
        table[pl.ds(pl.multiple_of(plane * 96 + n * 16, 16), 16), :] = beside(split2(g))


def constants(before, sign, after, mono_col):
    j, k = iota((512, 256), 0) & 255, iota((512, 256), 1)
    before[...] = jnp.where(j < k, 1.0, 0.0).astype(BF16)
    sign[...] = jnp.where(j < k, 1.0, jnp.where(j > k, -1.0, 0.0)).astype(BF16)
    after[...] = jnp.where(j > k, 1.0, 0.0).astype(BF16)
    col = iota((256, 128), 1)
    mono_col[...] = jnp.where(col < 24, monomials(iota((256, 128), 0), col & 7), 0.0).astype(BF16)


def composite(
    pos_ref, counts_ref, color_ref, normal_ref, loss_ref, table, grads, before, sign, after, mono_col
):
    lane = iota((1, 256), 1)
    row8 = iota((8, 256), 0)
    y_scale = jnp.where(row8 < 3, -0.25, jnp.where(row8 < 6, 1.0, 0.0))
    y_const = jnp.where(row8 == 6, 0.25, 0.0)
    kappa = 2.0 / 256.0
    dv_scale = jnp.where(row8 < 3, -0.25 * kappa, jnp.where(row8 < 6, kappa, 0.0))
    px_low = (row8.astype(F32) - 7.5) * 0.125
    px_high = px_low + 1.0
    zero1 = jnp.zeros((1, 256), F32)
    zero8 = jnp.zeros((8, 256), F32)

    def tiles(i, c):
        ts = [i * GROUP + u for u in range(GROUP)]
        each = range(GROUP)
        rows = []
        for t in ts:
            rows.append(look_up(table[...], pos_ref[pl.ds(t, 1), :], 24, 2))
        coefs, sigs = [], []
        for u, t in enumerate(ts):
            a0, a1, a2, b0, b1, b2, logit = [rows[u][r : r + 1] for r in range(7)]
            s = -0.5 * LOG2E
            grow = jnp.exp(-logit)
            offset = jnp.log(1.0 + grow) * (-LOG2E) + LOG2_TOP
            sigs.append(1.0 / (1.0 + grow))
            c0 = jnp.where(lane < counts_ref[t], s * (a0 * a0 + b0 * b0) + offset, -1e4)
            coef = stack(
                [
                    c0,
                    (2.0 * s) * (a0 * a1 + b0 * b1),
                    (2.0 * s) * (a0 * a2 + b0 * b2),
                    s * (a1 * a1 + b1 * b1),
                    (2.0 * s) * (a1 * a2 + b1 * b2),
                    s * (a2 * a2 + b2 * b2),
                    zero1,
                    zero1,
                ]
            )
            coefs.append(stack([p.astype(F32) for p in split3(coef)] + [zero8]).astype(BF16))
        depth = [rows[u][7:8] for u in each]
        v8 = [rows[u][8:16] for u in each]
        alpha = [jnp.exp2(dot_nn(mono_col[:, 0:32], coefs[u])) for u in each]
        logkeep = [jnp.log(1.0 - alpha[u]) for u in each]
        seen = unstack(
            dot_nn(stack([beside(split2(logkeep[u])) for u in each]), before[...]), 256, GROUP
        )
        w = [alpha[u] * jnp.exp(seen[u]) for u in each]
        w2 = [beside(split2(w[u])) for u in each]
        sums = unstack(
            dot_nn(stack(w2 + [beside(split2(w[u] * depth[u])) for u in each]), sign[...]),
            256,
            2 * GROUP,
        )
        am, bm = sums[0:GROUP], sums[GROUP:]
        resid, x32, y = [], [], []
        for u, t in enumerate(ts):
            v16 = stack([p.astype(F32) for p in split2(v8[u])]).astype(BF16)
            shown = dot_nt(beside([v16, v16]), w2[u])
            shown = shown[0:8] + shown[8:16]
            resid.append(shown[3:6] - color_ref[:, t, :])
        for u, t in enumerate(ts):
            x8 = stack([normal_ref[:, t, :], resid[u], zero1 + 1.0, zero1])
            xh, xl = [p.astype(F32) for p in split2(x8)]
            yh, yl = [p.astype(F32) for p in split2(v8[u] * y_scale + y_const)]
            x32.append(stack([xh, xl, xh, zero8]).astype(BF16))
            y32 = stack([yh, yh, yl, zero8]).astype(BF16)
            y.append((dot_tn(x32[u], y32) + (depth[u] * am[u] - bm[u])) * w[u])
        behind = unstack(
            dot_nn(stack([beside(split2(y[u])) for u in each]), after[...]), 256, GROUP
        )
        for u, t in enumerate(ts):
            hgrad = y[u] - behind[u] * (alpha[u] * jnp.exp(-logkeep[u]))
            low = [zero8] * 3
            high = [zero8] * 3
            for r in range(16):
                low[0] = low[0] + hgrad[r * 16 : r * 16 + 8]
                high[0] = high[0] + hgrad[r * 16 + 8 : r * 16 + 16]
                for n in (1, 2):
                    low[n] = low[n] + low[n - 1]
                    high[n] = high[n] + high[n - 1]

            def moment(first, second):
                return jnp.sum(first + second, axis=0, keepdims=True) * (-kappa)

            def rows_of(f):
                return f[0], 1.0625 * f[0] - 0.125 * f[1], (
                    1.12890625 * f[0] - 0.28125 * f[1] + 0.03125 * f[2]
                )

            low, high = rows_of(low), rows_of(high)
            m0 = moment(low[0], high[0])
            m1 = moment(low[0] * px_low, high[0] * px_high)
            m2 = moment(low[1], high[1])
            m3 = moment(low[0] * (px_low * px_low), high[0] * (px_high * px_high))
            m4 = moment(low[1] * px_low, high[1] * px_high)
            m5 = moment(low[2], high[2])
            x16 = x32[u][0:16]
            dv = dot_nn(beside([x16, x16]), stack([w2[u][:, 0:256], w2[u][:, 256:512]]))
            dv = dv[0:8] + dv[8:16]
            ga = jnp.sum(w[u] * am[u], axis=0, keepdims=True)
            a0, a1, a2, b0, b1, b2 = [rows[u][r : r + 1] for r in range(6)]
            out = stack(
                [
                    a0 * m0 + a1 * m1 + a2 * m2,
                    a0 * m1 + a1 * m3 + a2 * m4,
                    a0 * m2 + a1 * m4 + a2 * m5,
                    b0 * m0 + b1 * m1 + b2 * m2,
                    b0 * m1 + b1 * m3 + b2 * m4,
                    b0 * m2 + b1 * m4 + b2 * m5,
                    (sigs[u] - 1.0) * m0,
                    kappa * ga,
                    dv * dv_scale,
                ]
            )
            grads[pl.ds(pl.multiple_of(t * 16, 16), 16), :] = beside(split2(out))
            facing = v8[u][0:3] * dv[0:3]
            loss = (
                jnp.sum(resid[u] * resid[u] - 0.5 * facing, axis=0, keepdims=True)
                + 2.0 * (depth[u] * ga)
                + 0.5 * dv[6:7]
            ) * (1.0 / 256.0)
            loss_ref[pl.ds(t, 1), :] = loss[:, 0:128] + loss[:, 128:256]
        return c

    lax.fori_loop(0, TILES // GROUP, tiles, 0)


def return_rows(plane, slot_ref, out_ref, grads, between):
    index = plane_blocks(index_blocks, slot_ref, plane)
    write_plane(out_ref, plane, index, 32, grads[...], between)


def sum_rows(plane, back_ref, got_ref, acc, between):
    index = plane_blocks(index_blocks, got_ref, plane)
    data = plane_blocks(message_blocks, back_ref, plane)
    left, right = [], []
    for n, (i, d) in enumerate(zip(index, data)):
        between(n)
        hot = one_hot_rows(256, i & 255)
        both = beside([p.astype(F32) for p in split2(d)])
        high = beside([i >> 8, i >> 8])
        left.append(stack([jnp.where(high == h, both, 0.0).astype(BF16) for h in range(16)]))
        right += [hot, hot]
    acc[plane] = dot_nt(beside(left), beside(right))


def finish_grads(harmonics_ref, basis_ref, dirs_ref, mask_ref, tmp, gs_ref, gp_ref, gh_ref, acc):
    def finish(h, c):
        lanes = pl.ds(pl.multiple_of(h * 256, 256), 256)
        views = [acc[v, pl.ds(pl.multiple_of(h * 16, 16), 16), :] for v in range(4)]
        total = (views[0] + views[1]) + (views[2] + views[3])
        gs_ref[:, lanes] = total[0:11]
        dcol = [
            [views[v][11 + ch : 12 + ch] * mask_ref[ch * 4 + v : ch * 4 + v + 1, lanes] for v in range(4)]
            for ch in range(3)
        ]
        basis = [basis_ref[v, :, lanes] for v in range(4)]
        coeffs = [harmonics_ref[ch * 16 : ch * 16 + 16, lanes] for ch in range(3)]
        for ch in range(3):
            parts = [basis[v] * dcol[ch][v] for v in range(4)]
            gh_ref[ch * 16 : ch * 16 + 16, lanes] = (parts[0] + parts[1]) + (parts[2] + parts[3])
        for v in range(4):
            dbasis = coeffs[0] * dcol[0][v] + coeffs[1] * dcol[1][v] + coeffs[2] * dcol[2][v]
            for half in range(2):
                tmp[pl.ds(half * 128 + v, 16, stride=8), :] = dbasis[:, half * 128 : half * 128 + 128]
        x, y, z, inverse = [dirs_ref[d, :, lanes] for d in range(4)]
        grads = sh_basis_back(x, y, z, [row_of(tmp, b) for b in range(16)])
        along = grads[0] * x + grads[1] * y + grads[2] * z
        for d, n in enumerate((x, y, z)):
            gp_ref[d : d + 1, lanes] = jnp.sum(
                (grads[d] - n * along) * inverse, axis=0, keepdims=True
            )
        return c

    lax.fori_loop(0, 16, finish, 0)


def greet_all(me):
    barrier = pltpu.get_barrier_semaphore()

    def greet(i, c):
        for s in range(1, 16):
            pl.semaphore_signal(
                barrier, inc=1, device_id=(lax.rem(me + i * 15 + s, N_DEV),), device_id_type=MESH
            )
        return c

    lax.fori_loop(0, 8, greet, 0)
    for s in range(121, N_DEV):
        pl.semaphore_signal(
            barrier, inc=1, device_id=(lax.rem(me + s, N_DEV),), device_id_type=MESH
        )


def send_block(src_ref, dst_ref, me, peer, send_sem, recv_sem):
    pltpu.make_async_remote_copy(
        src_ref=src_ref.at[peer],
        dst_ref=dst_ref.at[me],
        send_sem=send_sem,
        recv_sem=recv_sem.at[me // 32],
        device_id=(peer,),
        device_id_type=MESH,
    ).start()


def blocks_of(ref, count, me, send_sem, recv_sem):
    return pltpu.make_async_remote_copy(
        src_ref=ref.at[pl.ds(0, count)],
        dst_ref=ref.at[pl.ds(0, count)],
        send_sem=send_sem,
        recv_sem=recv_sem,
        device_id=(me,),
        device_id_type=MESH,
    )


def plane_at(me, i, direction):
    distance = (1, 3, 2, 0)[i]
    return lax.rem(me // 32 + (distance if direction > 0 else (4 - distance) % 4), 4)


def plane_sender(src_ref, dst_ref, me, i, direction, send_sem, recv_sem):
    plane = plane_at(me, i, direction)

    def send(s):
        peer = plane * 32 + lax.rem(me % 32 + 1 + s, 32)
        send_block(src_ref, dst_ref, me, peer, send_sem, recv_sem)

    count = 31 if i == 3 else 32
    return send, count, plane


def between_of(sender):
    send, count, _ = sender

    def between(n):
        for s in range(n * 6, min(n * 6 + 6, count)):
            send(s)

    return between


def send_plane(sender):
    send, count, _ = sender

    def one(s, c):
        send(s)
        return c

    lax.fori_loop(0, count, one, 0)


def nothing(n):
    pass


def wait_plane(ref, me, i, direction, send_sem, recv_sem):
    plane = plane_at(me, i, direction)
    blocks_of(ref, 32 if i < 3 else 31, me, send_sem, recv_sem.at[plane]).wait_recv()
    return plane


def step_kernel(
    splat_hbm, position_hbm, harmonics_hbm, cams_hbm, lists_hbm, counts_hbm, color_hbm, normal_hbm,
    acc, basis, dirs, mask, loss_ref,
    splat_ref, position_ref, harmonics_ref, cams_ref, lists_ref, counts_ref, color_ref, normal_ref,
    ask, got, slot, pos, rows, recv, grad_rows, back, upper, surfels, table, grads,
    before, sign, after, mono_col, tmp, load_sem, send_sem, ask_sem, row_sem, back_sem,
):
    me = lax.axis_index("surf")
    pairs = [
        (lists_hbm, lists_ref), (counts_hbm, counts_ref), (cams_hbm, cams_ref),
        (position_hbm, position_ref), (harmonics_hbm, harmonics_ref), (splat_hbm, splat_ref),
        (color_hbm, color_ref), (normal_hbm, normal_ref),
    ]
    loads = [
        pltpu.make_async_copy(src, dst, load_sem.at[n]) for n, (src, dst) in enumerate(pairs)
    ]
    for load in loads:
        load.start()
    greet_all(me)
    loads[0].wait()
    loads[1].wait()
    route(lists_ref, counts_ref, ask, slot, pos, upper, nothing)
    pl.semaphore_wait(pltpu.get_barrier_semaphore(), N_DEV - 1)
    got[me] = ask[me]
    for load in loads[2:6]:
        load.wait()

    requests = [plane_sender(ask, got, me, i, 1, send_sem.at[0], ask_sem) for i in range(4)]

    def request(h, i):
        send, count, _ = requests[i]
        for s in range(8):
            send((h - 4 * i) * 8 + s)

    def request_own(h, i):
        send, count, _ = requests[i]
        for s in range(7):
            send((h - 4 * i) * 8 + s)

        @pl.when(h < 15)
        def _():
            send((h - 4 * i) * 8 + 7)

    build_rows(
        splat_ref, position_ref, harmonics_ref, cams_ref, surfels, basis, dirs, mask, tmp,
        lambda h, i: request_own(h, i) if i == 3 else request(h, i),
    )
    between = nothing
    for i in range(4):
        plane = wait_plane(got, me, i, -1, send_sem.at[0], ask_sem)
        fetch_rows(plane, got, rows, surfels, between)
        sender = plane_sender(rows, recv, me, i, -1, send_sem.at[1], row_sem)
        between = between_of(sender)
    send_plane(sender)
    recv[me] = rows[me]
    constants(before, sign, after, mono_col)
    for load in loads[6:8]:
        load.wait()
    for i in range(4):
        arrange_rows(wait_plane(recv, me, i, 1, send_sem.at[1], row_sem), recv, table)
    composite(
        pos, counts_ref, color_ref, normal_ref, loss_ref, table, grads, before, sign, after, mono_col
    )
    between = nothing
    for i in range(4):
        sender = plane_sender(grad_rows, back, me, i, 1, send_sem.at[2], back_sem)
        return_rows(sender[2], slot, grad_rows, grads, between)
        between = between_of(sender)
    back[me] = grad_rows[me]
    for i in range(4):
        plane = wait_plane(back, me, i, -1, send_sem.at[2], back_sem)
        sum_rows(plane, back, got, acc, between if i == 0 else nothing)
    for n, ref in enumerate((ask, rows, grad_rows)):
        blocks_of(ref, N_DEV - 1, me, send_sem.at[n], ask_sem.at[0]).wait_send()


def finish_kernel(
    harmonics_ref, basis, dirs, mask, acc, loss_ref, gs_ref, gp_ref, gh_ref, total_ref, tmp
):
    parts = stack([p.astype(F32) for p in split3(loss_ref[...])]).astype(BF16)
    sums = dot_nt(jnp.full((16, 128), 1.0, BF16), parts)
    total_ref[...] = sums[0:1, 0:32] + sums[0:1, 32:64] + sums[0:1, 64:96]
    finish_grads(harmonics_ref, basis, dirs, mask, tmp, gs_ref, gp_ref, gh_ref, acc)


VM = pl.BlockSpec(memory_space=pltpu.VMEM)
LIMIT = 62 * 1024 * 1024


def on_device(
    splat, position, harmonics, cameras, tile_lists, tile_counts, target_color, target_normal
):
    acc, basis, dirs, mask, loss = pl.pallas_call(
        step_kernel,
        out_shape=(
            jax.ShapeDtypeStruct((4, 256, 256), F32),
            jax.ShapeDtypeStruct((4, 16, SURF), F32),
            jax.ShapeDtypeStruct((4, 4, SURF), F32),
            jax.ShapeDtypeStruct((12, SURF), F32),
            jax.ShapeDtypeStruct((TILES, 128), F32),
        ),
        in_specs=[pl.BlockSpec(memory_space=pltpu.HBM)] * 8,
        out_specs=(VM,) * 5,
        scratch_shapes=[
            pltpu.VMEM((11, SURF), F32),
            pltpu.VMEM((3, SURF), F32),
            pltpu.VMEM((48, SURF), F32),
            pltpu.VMEM((4, 3), F32),
            pltpu.VMEM((TILES, 256), I32),
            pltpu.SMEM((TILES,), I32),
            pltpu.VMEM((3, TILES, 256), F32),
            pltpu.VMEM((3, TILES, 256), F32),
            pltpu.VMEM((N_DEV, 1, 128), I32),
            pltpu.VMEM((N_DEV, 1, 128), I32),
            pltpu.VMEM((N_DEV, 1, 128), I32),
            pltpu.VMEM((TILES, 256), I32),
            pltpu.VMEM((N_DEV, 8, 128), F32),
            pltpu.VMEM((N_DEV, 8, 128), F32),
            pltpu.VMEM((N_DEV, 8, 128), F32),
            pltpu.VMEM((N_DEV, 8, 128), F32),
            pltpu.VMEM((256, 384), BF16),
            pltpu.VMEM((4, 256, 512), BF16),
            pltpu.VMEM((384, 512), BF16),
            pltpu.VMEM((512, 512), BF16),
            pltpu.VMEM((512, 256), BF16),
            pltpu.VMEM((512, 256), BF16),
            pltpu.VMEM((512, 256), BF16),
            pltpu.VMEM((256, 128), BF16),
            pltpu.VMEM((256, 128), F32),
            pltpu.SemaphoreType.DMA((8,)),
            pltpu.SemaphoreType.DMA((3,)),
            pltpu.SemaphoreType.DMA((8,)),
            pltpu.SemaphoreType.DMA((8,)),
            pltpu.SemaphoreType.DMA((8,)),
        ],
        compiler_params=pltpu.CompilerParams(
            collective_id=0, has_side_effects=True, vmem_limit_bytes=LIMIT
        ),
        name="surfel_step",
    )(splat, position, harmonics, cameras, tile_lists, tile_counts, target_color, target_normal)
    gs, gp, gh, total = pl.pallas_call(
        finish_kernel,
        out_shape=(
            jax.ShapeDtypeStruct((11, SURF), F32),
            jax.ShapeDtypeStruct((3, SURF), F32),
            jax.ShapeDtypeStruct((48, SURF), F32),
            jax.ShapeDtypeStruct((1, TILES), F32),
        ),
        in_specs=[VM] * 6,
        out_specs=(VM,) * 4,
        scratch_shapes=[pltpu.VMEM((256, 128), F32)],
        compiler_params=pltpu.CompilerParams(vmem_limit_bytes=LIMIT),
        name="surfel_finish",
    )(harmonics, basis, dirs, mask, acc, loss)
    return gs, gp, gh, total.reshape(TILES)


def solution(mesh):
    return jax.shard_map(
        on_device,
        mesh=mesh,
        in_specs=(
            P(None, "surf"),
            P(None, "surf"),
            P(None, "surf"),
            P(),
            P("surf", None),
            P("surf"),
            P(None, "surf", None),
            P(None, "surf", None),
        ),
        out_specs=(P(None, "surf"), P(None, "surf"), P(None, "surf"), P("surf")),
        check_vma=False,
    )
```

```python
import functools

import jax
import jax.numpy as jnp
from jax import lax
from jax.experimental import pallas as pl
from jax.experimental.pallas import tpu as pltpu
from jax.sharding import PartitionSpec as P

F32 = jnp.float32
BF16 = jnp.bfloat16
I32 = jnp.int32
MESH = pl.DeviceIdType.MESH
N_DEV = 128
TILES = 32
SURF = 4096
SHARE = 48
LOG2E = 1.4426950408889634
LOG2_TOP = -0.07400058144377693
GROUP = 8

sh_zero = 0.28209479177387814
sh_one = 0.4886025119029199
sh_two = (
    1.0925484305920792,
    -1.0925484305920792,
    0.31539156525252005,
    -1.0925484305920792,
    0.5462742152960396,
)
sh_three = (
    -0.5900435899266435,
    2.890611442640554,
    -0.4570457994644658,
    0.3731763325901154,
    -0.4570457994644658,
    1.445305721320277,
    -0.5900435899266435,
)


def iota(shape, dim):
    return lax.broadcasted_iota(I32, shape, dim)


def dot_nn(a, b):
    return lax.dot_general(a, b, (((1,), (0,)), ((), ())), preferred_element_type=F32)


def dot_nt(a, b):
    return lax.dot_general(a, b, (((1,), (1,)), ((), ())), preferred_element_type=F32)


def dot_tn(a, b):
    return lax.dot_general(a, b, (((0,), (0,)), ((), ())), preferred_element_type=F32)


def split2(x):
    hi = x.astype(BF16)
    return hi, (x - hi.astype(F32)).astype(BF16)


def split3(x):
    hi = x.astype(BF16)
    rest = x - hi.astype(F32)
    mid = rest.astype(BF16)
    return hi, mid, (rest - mid.astype(F32)).astype(BF16)


def one_hot_rows(rows, index):
    return jnp.where(iota((rows, index.shape[1]), 0) == index, 1.0, 0.0).astype(BF16)


def directions(pos_rows, cams):
    offs = [pos_rows[d] - cams[:, d : d + 1] for d in range(3)]
    length = jnp.sqrt(offs[0] * offs[0] + offs[1] * offs[1] + offs[2] * offs[2])
    return [o / length for o in offs], length


def sh_basis(x, y, z):
    xx, yy, zz = x * x, y * y, z * z
    t, h = sh_two, sh_three
    return [
        jnp.full_like(x, sh_zero),
        -sh_one * y,
        sh_one * z,
        -sh_one * x,
        t[0] * (x * y),
        t[1] * (y * z),
        t[2] * (2.0 * zz - xx - yy),
        t[3] * (x * z),
        t[4] * (xx - yy),
        h[0] * (y * (3.0 * xx - yy)),
        h[1] * (x * y * z),
        h[2] * (y * (4.0 * zz - xx - yy)),
        h[3] * (z * (2.0 * zz - 3.0 * xx - 3.0 * yy)),
        h[4] * (x * (4.0 * zz - xx - yy)),
        h[5] * (z * (xx - yy)),
        h[6] * (x * (xx - 3.0 * yy)),
    ]


def sh_basis_back(x, y, z, d):
    xx, yy, zz = x * x, y * y, z * z
    xy, yz, xz = x * y, y * z, x * z
    t, h = sh_two, sh_three
    gx = (
        -sh_one * d[3] + t[0] * (y * d[4]) - (2.0 * t[2]) * (x * d[6]) + t[3] * (z * d[7])
        + (2.0 * t[4]) * (x * d[8]) + (6.0 * h[0]) * (xy * d[9]) + h[1] * (yz * d[10])
        - (2.0 * h[2]) * (xy * d[11]) - (6.0 * h[3]) * (xz * d[12])
        + h[4] * ((4.0 * zz - 3.0 * xx - yy) * d[13]) + (2.0 * h[5]) * (xz * d[14])
        + (3.0 * h[6]) * ((xx - yy) * d[15])
    )
    gy = (
        -sh_one * d[1] + t[0] * (x * d[4]) + t[1] * (z * d[5]) - (2.0 * t[2]) * (y * d[6])
        - (2.0 * t[4]) * (y * d[8]) + (3.0 * h[0]) * ((xx - yy) * d[9]) + h[1] * (xz * d[10])
        + h[2] * ((4.0 * zz - xx - 3.0 * yy) * d[11]) - (6.0 * h[3]) * (yz * d[12])
        - (2.0 * h[4]) * (xy * d[13]) - (2.0 * h[5]) * (yz * d[14]) - (6.0 * h[6]) * (xy * d[15])
    )
    gz = (
        sh_one * d[2] + t[1] * (y * d[5]) + (4.0 * t[2]) * (z * d[6]) + t[3] * (x * d[7])
        + h[1] * (xy * d[10]) + (8.0 * h[2]) * (yz * d[11])
        + h[3] * ((6.0 * zz - 3.0 * xx - 3.0 * yy) * d[12]) + (8.0 * h[4]) * (xz * d[13])
        + h[5] * ((xx - yy) * d[14])
    )
    return gx, gy, gz


def lane_of(x):
    return iota(x.shape, 1)


def join_eight(pieces):
    blocks = [jnp.zeros_like(pieces[0]) for _ in range(3)]
    for s, piece in enumerate(pieces):
        b, lo = divmod(SHARE * s, 128)
        lane = lane_of(piece)
        blocks[b] = jnp.where((lane >= lo) & (lane < lo + SHARE), piece, blocks[b])
        if lo + SHARE > 128:
            blocks[b + 1] = jnp.where(lane < lo + SHARE - 128, piece, blocks[b + 1])
    return blocks


def split_eight(blocks):
    pieces = []
    for s in range(8):
        b, lo = divmod(SHARE * s, 128)
        piece = pltpu.roll(blocks[b], 128 - lo, 1) if lo else blocks[b]
        if lo + SHARE > 128:
            piece = jnp.where(
                lane_of(piece) < 128 - lo, piece, pltpu.roll(blocks[b + 1], 128 - lo, 1)
            )
        pieces.append(piece)
    return pieces


def shift(x, amount):
    return pltpu.roll(x, amount % 128, 1) if amount % 128 else x


def index_blocks(ref, first):
    return join_eight([shift(ref[first + s], SHARE * s) for s in range(8)])


def message_blocks(ref, first):
    pieces = []
    for s in range(8):
        tile = jnp.concatenate([ref[first + s], jnp.zeros((1, 128), F32)], axis=0)
        pieces.append(
            jnp.concatenate([shift(tile, SHARE * s), shift(tile, SHARE * s + 64)], axis=0)
        )
    return join_eight(pieces)


def write_messages(ref, first, blocks):
    for s, piece in enumerate(split_eight(blocks)):
        ref[first + s] = jnp.where(
            lane_of(piece[0:8]) < 64, piece[0:8], pltpu.roll(piece[8:16], 64, 1)
        )[0:7]


def wide(blocks):
    return [
        jnp.concatenate(blocks[2 * i : 2 * i + 2], axis=1) for i in range(len(blocks) // 2)
    ]


def halves(chunks):
    return [c[:, 128 * i : 128 * i + 128] for c in chunks for i in range(2)]


def pick_rows(found, high, count):
    parts = [jnp.where(high == h, found[h * 16 : h * 16 + 16], 0.0) for h in range(count)]
    while len(parts) > 1:
        pairs = [parts[i] + parts[i + 1] for i in range(0, len(parts) - 1, 2)]
        parts = pairs + ([parts[-1]] if len(parts) % 2 else [])
    return parts[0]


def look_up(table, index, count, splits):
    hot = one_hot_rows(256, index & 255)
    found = dot_nn(table, jnp.concatenate([hot] * splits, axis=0))
    return pick_rows(found, index >> 8, count)


def tall(row):
    return jnp.concatenate([jnp.broadcast_to(row, (16, 256)).astype(BF16)] * (N_DEV // 16), axis=0)


def route(lists_ref, counts_ref, send_ref, slot_ref, pos_ref, upper, greet):
    col = iota((256, 384), 1)
    upper[...] = jnp.where((iota((256, 384), 0) < col) | (col > 255), 1.0, 0.0).astype(BF16)
    holder_id = iota((N_DEV, 256), 0)
    lane = iota((1, 256), 1)
    rank_id = iota((N_DEV, 256), 0) & 63
    group = 8

    def tiles(i, state, greets):
        carry, sums = state
        if greets:
            greet(i)
        flats = [lists_ref[pl.ds(i * group + u, 1), :] for u in range(group)]
        lives = [lane < counts_ref[i * group + u] for u in range(group)]
        holders = [jnp.where(lives[u], flats[u] // SURF, -1) for u in range(group)]
        ones = [jnp.where(holder_id == h, 1.0, 0.0) for h in holders]
        marks = [o.astype(BF16) for o in ones]
        counts = dot_nn(jnp.concatenate(marks, axis=0), upper[...])
        left, right = [], []
        for u in range(group):
            count = counts[u * N_DEV : u * N_DEV + N_DEV]
            rank = jnp.sum(
                ones[u] * (count[:, 0:256] + beside([carry, carry])), axis=0, keepdims=True
            ).astype(I32)
            carry = carry + count[:, 256:384]
            pos_ref[pl.ds(i * group + u, 1), :] = jnp.where(
                lives[u], holders[u] * SHARE + rank, -1
            )
            local = flats[u] % SURF
            values = [
                (local // 8 - 256).astype(F32),
                (local % 8 * TILES + (i * group + u)).astype(F32),
                lane.astype(F32),
            ]
            left.append(jnp.concatenate([marks[u] * tall(v) for v in values], axis=0))
            right.append(jnp.where(rank_id == rank, 1.0, 0.0).astype(BF16))
        sums = sums + dot_nt(jnp.concatenate(left, axis=1), jnp.concatenate(right, axis=1))
        return carry, sums

    state = (jnp.zeros((N_DEV, 128), F32), jnp.zeros((3 * N_DEV, 128), F32))
    state = lax.fori_loop(0, 2, lambda i, c: tiles(i, c, True), state)
    _, sums = lax.fori_loop(2, TILES // group, lambda i, c: tiles(i, c, False), state)
    named = (iota((N_DEV, 128), 1) & 63) < SHARE
    low = sums[128:256].astype(I32)
    local = (sums[0:128].astype(I32) + 256) * 8 + low // TILES
    slot = low % TILES * 256 + sums[256:384].astype(I32)
    send_ref[:, 0, :] = jnp.where(named, local, -1)
    slot_ref[:, 0, :] = jnp.where(named, slot, -1)


def put_row(tmp, b, value):
    for half in range(2):
        tmp[half * 128 + b * 8 : half * 128 + b * 8 + 4, :] = value[:, half * 128 : half * 128 + 128]


def row_of(tmp, b):
    return jnp.concatenate(
        [tmp[half * 128 + b * 8 : half * 128 + b * 8 + 4, :] for half in range(2)], axis=1
    )


def column(tmp, v):
    return jnp.concatenate(
        [tmp[pl.ds(half * 128 + v, 16, stride=8), :] for half in range(2)], axis=1
    )


def build_rows(
    splat_ref, position_ref, harmonics_ref, cams_ref, table, basis_ref, dirs_ref, mask_ref, tmp, request
):
    cams = cams_ref[...]

    def build(h, own):
        request(h, own)
        lanes = pl.ds(pl.multiple_of(h * 256, 256), 256)
        dirs, length = directions([position_ref[d : d + 1, lanes] for d in range(3)], cams)
        for d, value in enumerate(dirs + [1.0 / length]):
            dirs_ref[d, :, lanes] = value
        for b, value in enumerate(sh_basis(*dirs)):
            put_row(tmp, b, value)
        splat = splat_ref[:, lanes]
        coeffs = [harmonics_ref[ch * 16 : ch * 16 + 16, lanes] for ch in range(3)]
        for v in range(4):
            basis = column(tmp, v)
            basis_ref[v, :, lanes] = basis
            colors = []
            for ch in range(3):
                value = jnp.sum(coeffs[ch] * basis, axis=0, keepdims=True) + 0.5
                mask_ref[ch * 4 + v : ch * 4 + v + 1, lanes] = jnp.where(
                    value > 0.0, 1.0, jnp.where(value == 0.0, 0.5, 0.0)
                )
                colors.append(jnp.maximum(value, 0.0))
            zero = jnp.zeros((1, 256), F32)
            rows = jnp.concatenate([splat[0:7], zero, splat[7:11]] + colors + [zero], axis=0)
            table[v, pl.ds(pl.multiple_of(h * 16, 16), 16), :] = jnp.concatenate(split2(rows), axis=1)

    for i in range(4):
        lax.fori_loop(4 * i, 4 * i + 4, lambda h, c: build(h, i) or c, 0, unroll=True)


def plane_blocks(blocks_of_eight, ref, plane):
    return wide([b for s in range(4) for b in blocks_of_eight(ref, plane * 32 + s * 8)])


def write_plane(ref, plane, index, count, table, between):
    chunks = []
    for n, i in enumerate(index):
        chunks.append(look_up(table, i, count, 2))
        between(n)
    blocks = halves(chunks)
    for s in range(4):
        write_messages(ref, plane * 32 + s * 8, blocks[3 * s : 3 * s + 3])


def fetch_rows(plane, got_ref, out_ref, table, between):
    index = plane_blocks(index_blocks, got_ref, plane)
    write_plane(out_ref, plane, index, 16, table[plane], between)


def monomials(pixel, which):
    px = ((pixel & 15).astype(F32) - 7.5) * 0.125
    py = ((pixel >> 4).astype(F32) - 7.5) * 0.125
    m = jnp.where(which == 0, 1.0, 0.0)
    for n, value in ((1, px), (2, py), (3, px * px), (4, px * py), (5, py * py)):
        m = jnp.where(which == n, value, m)
    return m


def stack(parts):
    return jnp.concatenate(parts, axis=0)


def beside(parts):
    return jnp.concatenate(parts, axis=1)


def unstack(x, rows, count):
    return [x[rows * i : rows * i + rows] for i in range(count)]


def arrange_rows(plane, recv_ref, table):
    for n, g in enumerate(plane_blocks(message_blocks, recv_ref, plane)):
        table[pl.ds(pl.multiple_of(plane * 96 + n * 16, 16), 16), :] = beside(split2(g))


def constants(before, sign, after, mono_col, between):
    for n in range(4):
        rows = slice(n * 128, n * 128 + 128)
        j, k = (iota((128, 256), 0) + n * 128) & 255, iota((128, 256), 1)
        before[rows, :] = jnp.where(j < k, 1.0, 0.0).astype(BF16)
        sign[rows, :] = jnp.where(j < k, 1.0, jnp.where(j > k, -1.0, 0.0)).astype(BF16)
        after[rows, :] = jnp.where(j > k, 1.0, 0.0).astype(BF16)
        between(n)
    col = iota((256, 128), 1)
    between(4)
    mono_col[...] = jnp.where(col < 24, monomials(iota((256, 128), 0), col & 7), 0.0).astype(BF16)
    between(5)


def composite(
    pos_ref, counts_ref, color_ref, normal_ref, loss_ref, table, grads, before, sign, after, mono_col
):
    lane = iota((1, 256), 1)
    row8 = iota((8, 256), 0)
    normal_row = (row8 > 0) & (row8 < 4)
    color_row = (row8 > 3) & (row8 < 7)
    y_scale = jnp.where(normal_row, -0.25, jnp.where(color_row, 1.0, 0.0))
    y_const = jnp.where(row8 == 0, 0.25, 0.0)
    kappa = 2.0 / 256.0
    dv_scale = jnp.where(normal_row, -0.25 * kappa, jnp.where(color_row, kappa, 0.0))
    px_low = (row8.astype(F32) - 7.5) * 0.125
    px_high = px_low + 1.0
    zero1 = jnp.zeros((1, 256), F32)
    zero8 = jnp.zeros((8, 256), F32)

    def tiles(i, c):
        ts = [i * GROUP + u for u in range(GROUP)]
        each = range(GROUP)
        rows = []
        for t in ts:
            rows.append(look_up(table[...], pos_ref[pl.ds(t, 1), :], 24, 2))
        coefs, sigs = [], []
        for u, t in enumerate(ts):
            a0, a1, a2, b0, b1, b2, logit = [rows[u][r : r + 1] for r in range(7)]
            s = -0.5 * LOG2E
            grow = jnp.exp(-logit)
            offset = jnp.log(1.0 + grow) * (-LOG2E) + LOG2_TOP
            sigs.append(1.0 / (1.0 + grow))
            c0 = jnp.where(lane < counts_ref[t], s * (a0 * a0 + b0 * b0) + offset, -1e4)
            coef = stack(
                [
                    c0,
                    (2.0 * s) * (a0 * a1 + b0 * b1),
                    (2.0 * s) * (a0 * a2 + b0 * b2),
                    s * (a1 * a1 + b1 * b1),
                    (2.0 * s) * (a1 * a2 + b1 * b2),
                    s * (a2 * a2 + b2 * b2),
                    zero1,
                    zero1,
                ]
            )
            coefs.append(stack([p.astype(F32) for p in split3(coef)] + [zero8]).astype(BF16))
        depth = [rows[u][8:9] for u in each]
        v8 = [rows[u][8:16] for u in each]
        alpha = [jnp.exp2(dot_nn(mono_col[:, 0:32], coefs[u])) for u in each]
        logkeep = [jnp.log(1.0 - alpha[u]) for u in each]
        seen = unstack(
            dot_nn(stack([beside(split2(logkeep[u])) for u in each]), before[...]), 256, GROUP
        )
        w = [alpha[u] * jnp.exp(seen[u]) for u in each]
        w2 = [beside(split2(w[u])) for u in each]
        sums = unstack(
            dot_nn(stack(w2 + [beside(split2(w[u] * depth[u])) for u in each]), sign[...]),
            256,
            2 * GROUP,
        )
        am, bm = sums[0:GROUP], sums[GROUP:]
        resid, x32, y = [], [], []
        for u, t in enumerate(ts):
            v16 = stack([p.astype(F32) for p in split2(v8[u])]).astype(BF16)
            shown = dot_nt(beside([v16, v16]), w2[u])
            shown = shown[0:8] + shown[8:16]
            resid.append(shown[4:7] - color_ref[:, t, :])
        for u, t in enumerate(ts):
            x8 = stack([zero1 + 1.0, normal_ref[:, t, :], resid[u], zero1])
            xh, xl = [p.astype(F32) for p in split2(x8)]
            yh, yl = [p.astype(F32) for p in split2(v8[u] * y_scale + y_const)]
            x32.append(stack([xh, xl, xh, zero8]).astype(BF16))
            y32 = stack([yh, yh, yl, zero8]).astype(BF16)
            y.append((dot_tn(x32[u], y32) + (depth[u] * am[u] - bm[u])) * w[u])
        behind = unstack(
            dot_nn(stack([beside(split2(y[u])) for u in each]), after[...]), 256, GROUP
        )
        for u, t in enumerate(ts):
            hgrad = y[u] - behind[u] * (alpha[u] * jnp.exp(-logkeep[u]))
            low = [zero8] * 3
            high = [zero8] * 3
            for r in range(16):
                low[0] = low[0] + hgrad[r * 16 : r * 16 + 8]
                high[0] = high[0] + hgrad[r * 16 + 8 : r * 16 + 16]
                for n in (1, 2):
                    low[n] = low[n] + low[n - 1]
                    high[n] = high[n] + high[n - 1]

            def moment(first, second):
                return jnp.sum(first + second, axis=0, keepdims=True) * (-kappa)

            def rows_of(f):
                return f[0], 1.0625 * f[0] - 0.125 * f[1], (
                    1.12890625 * f[0] - 0.28125 * f[1] + 0.03125 * f[2]
                )

            low, high = rows_of(low), rows_of(high)
            m0 = moment(low[0], high[0])
            m1 = moment(low[0] * px_low, high[0] * px_high)
            m2 = moment(low[1], high[1])
            m3 = moment(low[0] * (px_low * px_low), high[0] * (px_high * px_high))
            m4 = moment(low[1] * px_low, high[1] * px_high)
            m5 = moment(low[2], high[2])
            x16 = x32[u][0:16]
            dv = dot_nn(beside([x16, x16]), stack([w2[u][:, 0:256], w2[u][:, 256:512]]))
            dv = dv[0:8] + dv[8:16]
            ga = jnp.sum(w[u] * am[u], axis=0, keepdims=True)
            a0, a1, a2, b0, b1, b2 = [rows[u][r : r + 1] for r in range(6)]
            out = stack(
                [
                    a0 * m0 + a1 * m1 + a2 * m2,
                    a0 * m1 + a1 * m3 + a2 * m4,
                    a0 * m2 + a1 * m4 + a2 * m5,
                    b0 * m0 + b1 * m1 + b2 * m2,
                    b0 * m1 + b1 * m3 + b2 * m4,
                    b0 * m2 + b1 * m4 + b2 * m5,
                    (sigs[u] - 1.0) * m0,
                    zero1,
                    dv * dv_scale + jnp.where(row8 == 0, kappa * ga, 0.0),
                ]
            )
            grads[pl.ds(pl.multiple_of(t * 16, 16), 16), :] = beside(split2(out))
            facing = v8[u][1:4] * dv[1:4]
            loss = (
                jnp.sum(resid[u] * resid[u] - 0.5 * facing, axis=0, keepdims=True)
                + 2.0 * (depth[u] * ga)
                + 0.5 * dv[0:1]
            ) * (1.0 / 256.0)
            loss_ref[pl.ds(t, 1), :] = loss[:, 0:128] + loss[:, 128:256]
        return c

    lax.fori_loop(0, TILES // GROUP, tiles, 0)


def return_rows(plane, slot_ref, out_ref, grads, between):
    index = plane_blocks(index_blocks, slot_ref, plane)
    write_plane(out_ref, plane, index, 32, grads[...], between)


def sum_rows(plane, back_ref, got_ref, acc, between):
    index = plane_blocks(index_blocks, got_ref, plane)
    data = plane_blocks(message_blocks, back_ref, plane)
    left, right = [], []
    for n, (i, d) in enumerate(zip(index, data)):
        between(n)
        hot = one_hot_rows(256, i & 255)
        both = beside([p.astype(F32) for p in split2(d)])
        high = beside([i >> 8, i >> 8])
        left.append(stack([jnp.where(high == h, both, 0.0).astype(BF16) for h in range(16)]))
        right += [hot, hot]
    acc[plane] = dot_nt(beside(left), beside(right))


def finish_grads(harmonics_ref, basis_ref, dirs_ref, mask_ref, tmp, gs_ref, gp_ref, gh_ref, acc):
    def finish(h, c):
        lanes = pl.ds(pl.multiple_of(h * 256, 256), 256)
        views = [acc[v, pl.ds(pl.multiple_of(h * 16, 16), 16), :] for v in range(4)]
        total = (views[0] + views[1]) + (views[2] + views[3])
        gs_ref[0:7, lanes] = total[0:7]
        gs_ref[7:11, lanes] = total[8:12]
        dcol = [
            [views[v][12 + ch : 13 + ch] * mask_ref[ch * 4 + v : ch * 4 + v + 1, lanes] for v in range(4)]
            for ch in range(3)
        ]
        basis = [basis_ref[v, :, lanes] for v in range(4)]
        coeffs = [harmonics_ref[ch * 16 : ch * 16 + 16, lanes] for ch in range(3)]
        for ch in range(3):
            parts = [basis[v] * dcol[ch][v] for v in range(4)]
            gh_ref[ch * 16 : ch * 16 + 16, lanes] = (parts[0] + parts[1]) + (parts[2] + parts[3])
        for v in range(4):
            dbasis = coeffs[0] * dcol[0][v] + coeffs[1] * dcol[1][v] + coeffs[2] * dcol[2][v]
            for half in range(2):
                tmp[pl.ds(half * 128 + v, 16, stride=8), :] = dbasis[:, half * 128 : half * 128 + 128]
        x, y, z, inverse = [dirs_ref[d, :, lanes] for d in range(4)]
        grads = sh_basis_back(x, y, z, [row_of(tmp, b) for b in range(16)])
        along = grads[0] * x + grads[1] * y + grads[2] * z
        for d, n in enumerate((x, y, z)):
            gp_ref[d : d + 1, lanes] = jnp.sum(
                (grads[d] - n * along) * inverse, axis=0, keepdims=True
            )
        return c

    lax.fori_loop(0, 16, finish, 0)


def greet_some(me, first, count):
    barrier = pltpu.get_barrier_semaphore()
    for n in range(count):
        pl.semaphore_signal(
            barrier, inc=1, device_id=(lax.rem(me + first + n, N_DEV),), device_id_type=MESH
        )


def send_block(src_ref, dst_ref, me, peer, send_sem, recv_sem):
    pltpu.make_async_remote_copy(
        src_ref=src_ref.at[peer],
        dst_ref=dst_ref.at[me],
        send_sem=send_sem,
        recv_sem=recv_sem.at[me // 32],
        device_id=(peer,),
        device_id_type=MESH,
    ).start()


def blocks_of(ref, count, me, send_sem, recv_sem):
    return pltpu.make_async_remote_copy(
        src_ref=ref.at[pl.ds(0, count)],
        dst_ref=ref.at[pl.ds(0, count)],
        send_sem=send_sem,
        recv_sem=recv_sem,
        device_id=(me,),
        device_id_type=MESH,
    )


def plane_at(me, i, direction):
    distance = (1, 3, 2, 0)[i]
    return lax.rem(me // 32 + (distance if direction > 0 else (4 - distance) % 4), 4)


def plane_sender(src_ref, dst_ref, me, i, direction, send_sem, recv_sem):
    plane = plane_at(me, i, direction)

    def send(s):
        peer = plane * 32 + lax.rem(me % 32 + 1 + s, 32)
        send_block(src_ref, dst_ref, me, peer, send_sem, recv_sem)

    count = 31 if i == 3 else 32
    return send, count, plane


def between_of(sender):
    send, count, _ = sender

    def between(n):
        for s in range(n * 6, min(n * 6 + 6, count)):
            send(s)

    return between


def nothing(n):
    pass


def wait_plane(ref, me, i, direction, send_sem, recv_sem):
    plane = plane_at(me, i, direction)
    blocks_of(ref, 32 if i < 3 else 31, me, send_sem, recv_sem.at[plane]).wait_recv()
    return plane


def step_kernel(
    splat_hbm, position_hbm, harmonics_hbm, cams_hbm, lists_hbm, counts_hbm, color_hbm, normal_hbm,
    acc_hbm, basis_hbm, dirs_hbm, mask_hbm, loss_ref,
    splat_ref, position_ref, harmonics_ref, cams_ref, lists_ref, counts_ref, color_ref, normal_ref,
    ask, got, slot, pos, rows, recv, grad_rows, back, upper, surfels, table, grads,
    before, sign, after, mono_col, tmp, acc, basis, dirs, mask,
    load_sem, send_sem, ask_sem, row_sem, back_sem, store_sem,
):
    me = lax.axis_index("surf")
    pairs = [
        (lists_hbm, lists_ref), (counts_hbm, counts_ref), (cams_hbm, cams_ref),
        (position_hbm, position_ref), (harmonics_hbm, harmonics_ref), (splat_hbm, splat_ref),
        (color_hbm, color_ref), (normal_hbm, normal_ref),
    ]
    loads = [
        pltpu.make_async_copy(src, dst, load_sem.at[n]) for n, (src, dst) in enumerate(pairs)
    ]
    for load in loads:
        load.start()
    greet_some(me, 127, 1)
    loads[0].wait()
    loads[1].wait()
    route(
        lists_ref, counts_ref, ask, slot, pos, upper, lambda i: greet_some(me, i * 63 + 1, 63)
    )
    pl.semaphore_wait(pltpu.get_barrier_semaphore(), N_DEV - 1)
    got[me] = ask[me]
    for load in loads[2:6]:
        load.wait()

    requests = [plane_sender(ask, got, me, i, 1, send_sem.at[0], ask_sem) for i in range(4)]

    def request(h, i):
        send, count, _ = requests[i]
        for s in range(8):
            send((h - 4 * i) * 8 + s)

    def request_own(h, i):
        send, count, _ = requests[i]
        for s in range(7):
            send((h - 4 * i) * 8 + s)

        @pl.when(h < 15)
        def _():
            send((h - 4 * i) * 8 + 7)

    build_rows(
        splat_ref, position_ref, harmonics_ref, cams_ref, surfels, basis, dirs, mask, tmp,
        lambda h, i: request_own(h, i) if i == 3 else request(h, i),
    )
    stores = [
        pltpu.make_async_copy(src, dst, store_sem.at[n])
        for n, (src, dst) in enumerate(((basis, basis_hbm), (dirs, dirs_hbm), (mask, mask_hbm)))
    ]
    for store in stores:
        store.start()
    between = nothing
    for i in range(4):
        plane = wait_plane(got, me, i, -1, send_sem.at[0], ask_sem)
        fetch_rows(plane, got, rows, surfels, between)
        sender = plane_sender(rows, recv, me, i, -1, send_sem.at[1], row_sem)
        between = between_of(sender)
    recv[me] = rows[me]
    constants(before, sign, after, mono_col, between)
    for load in loads[6:8]:
        load.wait()
    for i in range(4):
        arrange_rows(wait_plane(recv, me, i, 1, send_sem.at[1], row_sem), recv, table)
    composite(
        pos, counts_ref, color_ref, normal_ref, loss_ref, table, grads, before, sign, after, mono_col
    )
    between = nothing
    for i in range(4):
        sender = plane_sender(grad_rows, back, me, i, 1, send_sem.at[2], back_sem)
        return_rows(sender[2], slot, grad_rows, grads, between)
        between = between_of(sender)
    back[me] = grad_rows[me]
    for i in range(4):
        plane = wait_plane(back, me, i, -1, send_sem.at[2], back_sem)
        sum_rows(plane, back, got, acc, between if i == 0 else nothing)
        stores.append(pltpu.make_async_copy(acc.at[plane], acc_hbm.at[plane], store_sem.at[3 + i]))
        stores[-1].start()
    for n, ref in enumerate((ask, rows, grad_rows)):
        blocks_of(ref, N_DEV - 1, me, send_sem.at[n], ask_sem.at[0]).wait_send()
    for store in stores:
        store.wait()


def finish_kernel(
    harmonics_ref, basis, dirs, mask, acc, loss_ref, gs_ref, gp_ref, gh_ref, total_ref, tmp
):
    parts = stack([p.astype(F32) for p in split3(loss_ref[...])]).astype(BF16)
    sums = dot_nt(jnp.full((16, 128), 1.0, BF16), parts)
    total_ref[...] = sums[0:1, 0:32] + sums[0:1, 32:64] + sums[0:1, 64:96]
    finish_grads(harmonics_ref, basis, dirs, mask, tmp, gs_ref, gp_ref, gh_ref, acc)


VM = pl.BlockSpec(memory_space=pltpu.VMEM)
LIMIT = 62 * 1024 * 1024


def on_device(
    splat, position, harmonics, cameras, tile_lists, tile_counts, target_color, target_normal
):
    acc, basis, dirs, mask, loss = pl.pallas_call(
        step_kernel,
        out_shape=(
            jax.ShapeDtypeStruct((4, 256, 256), F32),
            jax.ShapeDtypeStruct((4, 16, SURF), F32),
            jax.ShapeDtypeStruct((4, 4, SURF), F32),
            jax.ShapeDtypeStruct((12, SURF), F32),
            jax.ShapeDtypeStruct((TILES, 128), F32),
        ),
        in_specs=[pl.BlockSpec(memory_space=pltpu.HBM)] * 8,
        out_specs=(pl.BlockSpec(memory_space=pltpu.HBM),) * 4 + (VM,),
        scratch_shapes=[
            pltpu.VMEM((11, SURF), F32),
            pltpu.VMEM((3, SURF), F32),
            pltpu.VMEM((48, SURF), F32),
            pltpu.VMEM((4, 3), F32),
            pltpu.VMEM((TILES, 256), I32),
            pltpu.SMEM((TILES,), I32),
            pltpu.VMEM((3, TILES, 256), F32),
            pltpu.VMEM((3, TILES, 256), F32),
            pltpu.VMEM((N_DEV, 1, 128), I32),
            pltpu.VMEM((N_DEV, 1, 128), I32),
            pltpu.VMEM((N_DEV, 1, 128), I32),
            pltpu.VMEM((TILES, 256), I32),
            pltpu.VMEM((N_DEV, 7, 128), F32),
            pltpu.VMEM((N_DEV, 7, 128), F32),
            pltpu.VMEM((N_DEV, 7, 128), F32),
            pltpu.VMEM((N_DEV, 7, 128), F32),
            pltpu.VMEM((256, 384), BF16),
            pltpu.VMEM((4, 256, 512), BF16),
            pltpu.VMEM((384, 512), BF16),
            pltpu.VMEM((512, 512), BF16),
            pltpu.VMEM((512, 256), BF16),
            pltpu.VMEM((512, 256), BF16),
            pltpu.VMEM((512, 256), BF16),
            pltpu.VMEM((256, 128), BF16),
            pltpu.VMEM((256, 128), F32),
            pltpu.VMEM((4, 256, 256), F32),
            pltpu.VMEM((4, 16, SURF), F32),
            pltpu.VMEM((4, 4, SURF), F32),
            pltpu.VMEM((12, SURF), F32),
            pltpu.SemaphoreType.DMA((8,)),
            pltpu.SemaphoreType.DMA((3,)),
            pltpu.SemaphoreType.DMA((8,)),
            pltpu.SemaphoreType.DMA((8,)),
            pltpu.SemaphoreType.DMA((8,)),
            pltpu.SemaphoreType.DMA((7,)),
        ],
        compiler_params=pltpu.CompilerParams(
            collective_id=0, has_side_effects=True, vmem_limit_bytes=LIMIT
        ),
        name="surfel_step",
    )(splat, position, harmonics, cameras, tile_lists, tile_counts, target_color, target_normal)
    gs, gp, gh, total = pl.pallas_call(
        finish_kernel,
        out_shape=(
            jax.ShapeDtypeStruct((11, SURF), F32),
            jax.ShapeDtypeStruct((3, SURF), F32),
            jax.ShapeDtypeStruct((48, SURF), F32),
            jax.ShapeDtypeStruct((1, TILES), F32),
        ),
        in_specs=[VM] * 6,
        out_specs=(VM,) * 4,
        scratch_shapes=[pltpu.VMEM((256, 128), F32)],
        compiler_params=pltpu.CompilerParams(vmem_limit_bytes=LIMIT),
        name="surfel_finish",
    )(harmonics, basis, dirs, mask, acc, loss)
    return gs, gp, gh, total.reshape(TILES)


def solution(mesh):
    return jax.shard_map(
        on_device,
        mesh=mesh,
        in_specs=(
            P(None, "surf"),
            P(None, "surf"),
            P(None, "surf"),
            P(),
            P("surf", None),
            P("surf"),
            P(None, "surf", None),
            P(None, "surf", None),
        ),
        out_specs=(P(None, "surf"), P(None, "surf"), P(None, "surf"), P("surf")),
        check_vma=False,
    )
```
